512 devices in a mesh: epoch: 16 (over x, y), tile: 32 (over z, core).
Axes of the slice: x: 4, y: 4, z: 16, core: 2. Of those that a mesh axis runs over, the one named last changes fastest.
Arguments:
- anomaly: bfloat16 [64, 3072, 2048], P('epoch', 'tile'), may hold values from -120 to 120
- mask: int32 [64, 3072, 2048], P('epoch', 'tile'), may hold values 0 or 1
- epoch_weight: float32 [64], replicated, may hold values from 0.25 to 4
- days: int32 [64], replicated, may hold values from 0 to 3652
- window: int32 [32, 16], P('tile', 'epoch'), may hold values from 1 to 16, as said below
Outputs:
- rate: float32 [3072, 2048], P('tile', 'epoch')
- curvature: float32 [3, 3072, 2048], P(None, 'tile', 'epoch')
The draws below stay inside these ranges and needn't reach their ends.
Inputs may be any that keep to these rules, and one draw needn't show every extreme that they name: `window`: one half-width for each block of the region; some block has 16.
All inputs are finite; a program needn't handle non-finite values. No bound on the sum of `mask` on one device may be relied on, other than what follows from the above.
Results may differ from the reference program's by a relative error of at most 0.0027.
Values may be sent and summed in bfloat16 or wider, within the bound.
No kernel may reach another device: no remote copies, remote signals or barrier semaphores. Data moves between devices by JAX's collectives and lax.ppermute only.
A program may use at most 64 MiB of HBM per device.

```python
import math
import jax
import jax.numpy as jnp
from jax import lax

EPOCHS = 64
MAXH = 16
RB = 96
CB = 128
NR = 3072
NC = 2048
N_EPOCH = 16
N_TILE = 32


def draw_window(key, part):
    key = jax.random.fold_in(key, 11)
    first_key, second_key = jax.random.split(key)
    blocks = N_TILE * N_EPOCH
    halves = jax.random.randint(first_key, (blocks,), 1, MAXH + 1)
    chosen = jax.random.randint(second_key, (), 0, blocks)
    halves = jnp.where(jnp.arange(blocks) == chosen, MAXH, halves)
    return halves.reshape(N_TILE, N_EPOCH).astype(jnp.int32)


def plant(result, key, least, high):
    longest = result.shape.index(max(result.shape))
    spots = []
    for shift in (0, 1):
        where = [jax.random.randint(jax.random.fold_in(key, axis), (), 0, length) for axis, length in enumerate(result.shape)]
        where[longest] = (where[longest] + shift) % result.shape[longest]
        spots.append(tuple(where))
    return result.at[spots[0]].set(least).at[spots[1]].set(high)


def block_scale(key, dims, cuts, low, largest):
    def one(position, shards_of):
        draws = jax.random.uniform(jax.random.fold_in(jax.random.fold_in(key, 6), position), (shards_of,), jnp.float32, low / len(cuts), largest / len(cuts))
        return jnp.repeat(jnp.exp(draws), dims[position] // shards_of).reshape((-1,) + (1,) * (len(dims) - position - 1))

    level = one(*cuts[0])
    for cut in cuts[1:]:
        level = level * one(*cut)
    return level


def centred(key, shape, deviation, most, pieces=(), kind=jnp.bfloat16):
    values = deviation * jax.random.normal(key, shape, jnp.float32)
    if pieces:
        values = values * block_scale(key, shape, pieces, -0.22, 0.18)
    return jnp.clip(values, -most, most).astype(kind)


def setup_inputs(seed: int = 0) -> dict:
    key_of = jax.random.split(jax.random.key(seed), 6)
    anomaly = centred(key_of[0], (EPOCHS, NR, NC), 20.0, 120.0, ((0, 16), (1, 32)))
    mask = plant((jax.random.randint(key_of[1], (EPOCHS, NR, NC), 0, 4) < 3).astype(jnp.int32), jax.random.fold_in(key_of[1], 1), 0, 1)
    epoch_weight = jnp.clip(jnp.exp(jax.random.uniform(key_of[2], (EPOCHS,), jnp.float32, math.log(0.25), math.log(4.0))), 0.25, 4.0)
    days = plant(jax.random.randint(key_of[3], (EPOCHS,), 0, 3653), jax.random.fold_in(key_of[3], 1), 0, 3652).astype(jnp.int32)
    window = draw_window(jax.random.fold_in(key_of[5], 71), 0)
    return dict(anomaly=anomaly, mask=mask, epoch_weight=epoch_weight, days=days, window=window)


def tap_values(offset, width):
    inside = (jnp.abs(offset) <= width).astype(jnp.float32)
    scaled = offset / width
    middle = (width + 1.0) / (3.0 * width)
    return inside, inside * scaled, inside * (scaled * scaled - middle)


def fit_window(padded, half):
    width = half.astype(jnp.float32)
    rows = padded.shape[0] - 2 * MAXH
    cols = padded.shape[1] - 2 * MAXH
    taps = jnp.arange(-MAXH, MAXH + 1).astype(jnp.float32)
    flat, slope, bowl = tap_values(taps, width)
    count = 2.0 * width + 1.0
    slope_norm = jnp.sum(slope * slope)
    bowl_norm = jnp.sum(bowl * bowl)
    across = (jnp.arange(cols + 2 * MAXH)[:, None] - jnp.arange(cols)[None, :] - MAXH).astype(jnp.float32)
    across_flat, across_slope, across_bowl = tap_values(across, width)
    along = (jnp.arange(rows + 2 * MAXH)[None, :] - jnp.arange(rows)[:, None] - MAXH).astype(jnp.float32)
    along_flat, along_slope, along_bowl = tap_values(along, width)
    highest = lax.Precision.HIGHEST
    row_flat = jnp.dot(padded, across_flat, precision=highest, preferred_element_type=jnp.float32)
    row_slope = jnp.dot(padded, across_slope, precision=highest, preferred_element_type=jnp.float32)
    row_bowl = jnp.dot(padded, across_bowl, precision=highest, preferred_element_type=jnp.float32)
    second_x = jnp.dot(along_flat, row_bowl, precision=highest, preferred_element_type=jnp.float32) * (2.0 / (count * bowl_norm))
    second_y = jnp.dot(along_bowl, row_flat, precision=highest, preferred_element_type=jnp.float32) * (2.0 / (count * bowl_norm))
    mixed = jnp.dot(along_slope, row_slope, precision=highest, preferred_element_type=jnp.float32) / (slope_norm * slope_norm)
    return jnp.stack([second_x, second_y, mixed])


def reference(anomaly, mask, epoch_weight, days, window):
    tau = (days.astype(jnp.float32) - 1826.5) / 365.25

    def accumulate(totals, item):
        level, valid, quality, moment = item
        rounded = (valid.astype(jnp.float32) * quality).astype(jnp.bfloat16)
        heavy = lax.optimization_barrier(rounded).astype(jnp.float32)
        loaded = heavy * level.astype(jnp.float32)
        return (totals[0] + heavy, totals[1] + heavy * moment, totals[2] + heavy * moment * moment,
                totals[3] + loaded, totals[4] + loaded * moment), None

    blank = jnp.zeros(anomaly.shape[1:], jnp.float32)
    sums, unused = lax.scan(accumulate, (blank, blank, blank, blank, blank), (anomaly, mask, epoch_weight, tau))
    lifted = sums[0] + 1.0
    rate = (lifted * sums[4] - sums[1] * sums[3]) / (lifted * (sums[2] + 1.0) - sums[1] * sums[1])
    padded = jnp.pad(rate, MAXH)

    def one_block(index):
        row_block = index // N_EPOCH
        col_block = index % N_EPOCH
        piece = lax.dynamic_slice(padded, ((row_block * RB).astype(jnp.int32), (col_block * CB).astype(jnp.int32)),
                                  (RB + 2 * MAXH, CB + 2 * MAXH))
        return fit_window(piece, window[row_block, col_block])

    blocks = lax.map(one_block, jnp.arange(N_TILE * N_EPOCH).astype(jnp.int32))
    curvature = blocks.reshape(N_TILE, N_EPOCH, 3, RB, CB).transpose(2, 0, 3, 1, 4).reshape(3, N_TILE * RB, N_EPOCH * CB)
    return rate, curvature
```

```python
import functools

import jax
import jax.numpy as jnp
from jax import lax
from jax.experimental import pallas as pl
from jax.experimental.pallas import tpu as pltpu
from jax.sharding import PartitionSpec as P

MAXH = 16
SIDE = 4
OWN = 4
ROWS = 96
COLS = 128
TILES = 32
AXES = ("epoch", "tile")
STEPS = (2, 1, -1)
ANY = pl.BlockSpec(memory_space=pl.ANY)
SMEM = pl.BlockSpec(memory_space=pltpu.SMEM)
VMEM = pl.BlockSpec(memory_space=pltpu.VMEM)
HBM = pl.BlockSpec(memory_space=pltpu.HBM)
LIMIT = pltpu.CompilerParams(vmem_limit_bytes=8 << 20)
STRIP = 16


def ring_pairs(step, first):
    pairs = []
    for x in range(SIDE):
        for y in range(SIDE):
            for tile in range(TILES):
                if (tile % 2 == 0) == first:
                    there = (x + step) % SIDE * SIDE + y
                else:
                    there = x * SIDE + (y + step) % SIDE
                pairs.append(((x * SIDE + y) * TILES + tile, there * TILES + tile))
    return pairs


def shift(values, step, first):
    return lax.ppermute(values, AXES, ring_pairs(step, first))


def place():
    spot = lax.axis_index("epoch")
    even = lax.axis_index("tile") % 2 == 0
    x, y = spot // SIDE, spot % SIDE
    return jnp.where(even, x, y), jnp.where(even, y, x), even


def block_of(even, first, second):
    return jnp.where(even, SIDE * first + second, SIDE * second + first)


def epoch_of(even, first, second):
    return block_of(even, first, second) * OWN


def columns(block):
    return pl.ds(pl.multiple_of(block * COLS, COLS), COLS)


def pack_kernel(step, quality, anomaly, mask, out, valid, sems):
    first, second, even = place()
    there = (first + step + SIDE) % SIDE
    copies = []
    for slot in range(SIDE):
        cols = columns(block_of(even, there, slot))
        copies.append(
            (
                pltpu.make_async_copy(anomaly.at[:, :, cols], out.at[slot, pl.ds(0, OWN)], sems.at[slot, 0]),
                pltpu.make_async_copy(mask.at[:, :, cols], valid.at[slot], sems.at[slot, 1]),
            )
        )
    for level, seen in copies:
        seen.start()
    for level, seen in copies:
        level.start()
    base = epoch_of(even, first, second)
    for slot in range(SIDE):
        copies[slot][1].wait()
        for own in range(OWN):
            out[slot, OWN + own] = (valid[slot, own].astype(jnp.float32) * quality[base + own]).astype(jnp.bfloat16)
    for level, seen in copies:
        level.wait()


def pack(step, quality, anomaly, mask):
    return pl.pallas_call(
        functools.partial(pack_kernel, step),
        out_shape=jax.ShapeDtypeStruct((SIDE, 2 * OWN, ROWS, COLS), jnp.bfloat16),
        in_specs=[SMEM, HBM, HBM] if step == STEPS[0] else [SMEM, ANY, ANY],
        out_specs=VMEM,
        scratch_shapes=[
            pltpu.VMEM((SIDE, OWN, ROWS, COLS), jnp.int32),
            pltpu.SemaphoreType.DMA((SIDE, 2)),
        ],
        compiler_params=LIMIT,
        cost_estimate=pl.CostEstimate(flops=1 << 20, bytes_accessed=3 << 20, transcendentals=0),
        name="pack",
    )(quality, anomaly, mask)


def added(totals, heavy, height, moment):
    timed = heavy * moment
    loaded = heavy * height
    terms = (heavy, timed, timed * moment, loaded, loaded * moment)
    return terms if totals is None else tuple(map(jnp.add, totals, terms))


def moments_of(tau, even, first, second):
    base = epoch_of(even, first, second)
    return [tau[base + own] for own in range(OWN)]


def early_kernel(quality, tau, anomaly, mask, got, out, level, valid, sems):
    first, second, even = place()
    copies = []
    for slot in range(SIDE):
        cols = columns(block_of(even, first, slot))
        copies.append(pltpu.make_async_copy(anomaly.at[:, :, cols], level.at[slot], sems.at[slot, 0]))
        copies.append(pltpu.make_async_copy(mask.at[:, :, cols], valid.at[slot], sems.at[slot, 1]))
    for copy in copies:
        copy.start()
    for copy in copies:
        copy.wait()
    base = epoch_of(even, first, second)
    own_quality = [quality[base + own] for own in range(OWN)]
    own_moments = moments_of(tau, even, first, second)
    got_moments = moments_of(tau, even, (first - STEPS[0] + SIDE) % SIDE, second)
    for slot in range(SIDE):

        def rows(index, carry):
            at = pl.ds(pl.multiple_of(index * STRIP, STRIP), STRIP)
            totals = None
            for own in range(OWN):
                heavy = (valid[slot, own, at].astype(jnp.float32) * own_quality[own]).astype(jnp.bfloat16)
                height = level[slot, own, at].astype(jnp.float32)
                totals = added(totals, heavy.astype(jnp.float32), height, own_moments[own])
            for own in range(OWN):
                heavy = got[slot, OWN + own, at].astype(jnp.float32)
                height = got[slot, own, at].astype(jnp.float32)
                totals = added(totals, heavy, height, got_moments[own])
            for which, total in enumerate(totals):
                out[slot, which, at] = total
            return carry

        lax.fori_loop(0, ROWS // STRIP, rows, 0)


def early_sums(quality, tau, anomaly, mask, got):
    return pl.pallas_call(
        early_kernel,
        out_shape=jax.ShapeDtypeStruct((SIDE, 5, ROWS, COLS), jnp.float32),
        in_specs=[SMEM, SMEM, ANY, ANY, VMEM],
        out_specs=VMEM,
        scratch_shapes=[
            pltpu.VMEM((SIDE, OWN, ROWS, COLS), jnp.bfloat16),
            pltpu.VMEM((SIDE, OWN, ROWS, COLS), jnp.int32),
            pltpu.SemaphoreType.DMA((SIDE, 2)),
        ],
        compiler_params=LIMIT,
        cost_estimate=pl.CostEstimate(flops=1 << 23, bytes_accessed=3 << 20, transcendentals=0),
        name="early",
    )(quality, tau, anomaly, mask, got)


def late_kernel(step, tau, early, got_b, got_c, out):
    first, second, even = place()
    slot = (second + step + SIDE) % SIDE
    moments = [moments_of(tau, even, (first - moved + SIDE) % SIDE, second) for moved in STEPS[1:]]

    def rows(index, carry):
        at = pl.ds(pl.multiple_of(index * STRIP, STRIP), STRIP)
        totals = tuple(early[slot, which, at] for which in range(5))
        for got, moment in zip((got_b, got_c), moments):
            for own in range(OWN):
                heavy = got[slot, OWN + own, at].astype(jnp.float32)
                height = got[slot, own, at].astype(jnp.float32)
                totals = added(totals, heavy, height, moment[own])
        for which, total in enumerate(totals):
            out[which, at] = total
        return carry

    lax.fori_loop(0, ROWS // STRIP, rows, 0)


def late_sums(step, tau, early, got_b, got_c):
    return pl.pallas_call(
        functools.partial(late_kernel, step),
        out_shape=jax.ShapeDtypeStruct((5, ROWS, COLS), jnp.float32),
        in_specs=[SMEM, VMEM, VMEM, VMEM],
        out_specs=VMEM,
        compiler_params=LIMIT,
        cost_estimate=pl.CostEstimate(flops=1 << 21, bytes_accessed=1 << 20, transcendentals=0),
        name="late",
    )(tau, early, got_b, got_c)


GROUPS = ROWS // MAXH


def lane(shape):
    return lax.broadcasted_iota(jnp.int32, shape, 1)


def rate_kernel(own, got_a, got_b, got_c, rate, head, tail):
    total = [own[i] + got_a[i] + got_b[i] + got_c[i] for i in range(5)]
    lifted = total[0] + 1.0
    value = (lifted * total[4] - total[1] * total[3]) / (lifted * (total[2] + 1.0) - total[1] * total[1])
    rate[...] = value
    place_of = lane((MAXH, COLS)) // MAXH
    left = jnp.zeros((MAXH, COLS), jnp.float32)
    right = jnp.zeros((MAXH, COLS), jnp.float32)
    for group in range(GROUPS):
        piece = value[group * MAXH : (group + 1) * MAXH]
        here = place_of == group
        left = jnp.where(here, pltpu.roll(piece, group * MAXH, 1) if group else piece, left)
        right = jnp.where(here, pltpu.roll(piece, (group + 1) * MAXH, 1), right)
    head[...] = left
    tail[...] = right


def fitted_rate(own, got):
    strip = jax.ShapeDtypeStruct((MAXH, COLS), jnp.float32)
    return pl.pallas_call(
        rate_kernel,
        out_shape=(jax.ShapeDtypeStruct((ROWS, COLS), jnp.float32), strip, strip),
        in_specs=[VMEM] * 4,
        out_specs=(VMEM, VMEM, VMEM),
        compiler_params=LIMIT,
        name="rate",
    )(own, *got)


def sides_kernel(rate, before, after, sides, top, bottom):
    place_of = lane((MAXH, COLS)) // MAXH
    for group in range(GROUPS):
        back = (COLS - group * MAXH) % COLS
        left = pltpu.roll(before[...], back, 1) if back else before[...]
        right = pltpu.roll(after[...], (back + MAXH) % COLS, 1)
        piece = jnp.where(place_of == 0, left, jnp.where(place_of == 1, right, 0.0))
        sides[pl.ds(group * MAXH, MAXH)] = piece
        if group == 0:
            top[pl.ds(MAXH, MAXH)] = piece
        if group == GROUPS - 1:
            bottom[pl.ds(MAXH, MAXH)] = piece
    top[pl.ds(0, MAXH)] = rate[pl.ds(0, MAXH)]
    bottom[pl.ds(0, MAXH)] = rate[pl.ds(ROWS - MAXH, MAXH)]


def with_sides(rate, before, after):
    edge = jax.ShapeDtypeStruct((2 * MAXH, COLS), jnp.float32)
    return pl.pallas_call(
        sides_kernel,
        out_shape=(jax.ShapeDtypeStruct((ROWS, COLS), jnp.float32), edge, edge),
        in_specs=[VMEM] * 3,
        out_specs=(VMEM, VMEM, VMEM),
        compiler_params=LIMIT,
        name="sides",
    )(rate, before, after)


def three_parts(values):
    high = values.astype(jnp.bfloat16)
    rest = values - high.astype(jnp.float32)
    middle = rest.astype(jnp.bfloat16)
    low = (rest - middle.astype(jnp.float32)).astype(jnp.bfloat16)
    return high, middle, low


def taps(offset, half):
    inside = jnp.abs(offset) <= half
    flat = jnp.where(inside, 1.0, 0.0)
    slope = jnp.where(inside, offset, 0).astype(jnp.float32)
    return tuple(v.astype(jnp.bfloat16) for v in (flat, slope, slope * slope))


def product(left, right):
    return jnp.dot(left, right, preferred_element_type=jnp.float32)


def curve_kernel(window, rate, sides, above, below, out):
    half = window[0, 0]
    middle = (half * (half + 1)).astype(jnp.float32) / 3.0
    line = lax.broadcasted_iota(jnp.int32, (2 * COLS, COLS), 0)
    column = jnp.where(
        line < COLS, line,
        jnp.where(line < COLS + MAXH, line - COLS - MAXH, jnp.where(line < COLS + 2 * MAXH, line - MAXH, 4 * COLS)),
    )
    across = jnp.concatenate(taps(column - lane((2 * COLS, COLS)), half), axis=1)
    tall = ROWS + 2 * MAXH
    spot = lane((ROWS, tall))
    row = jnp.where(spot < ROWS, spot, jnp.where(spot < ROWS + MAXH, spot - ROWS - MAXH, spot - MAXH))
    along = taps(row - lax.broadcasted_iota(jnp.int32, (ROWS, tall), 0), half)

    main = jnp.concatenate([rate[...], above[pl.ds(0, MAXH)], below[pl.ds(0, MAXH)]], axis=0)
    beside = jnp.concatenate([sides[...], above[pl.ds(MAXH, MAXH)], below[pl.ds(MAXH, MAXH)]], axis=0)
    parts = three_parts(jnp.concatenate([main, beside], axis=1))
    wide = product(parts[0], across) + product(parts[1], across) + product(parts[2], across)
    flat, slope, square = (wide[:, i * COLS : (i + 1) * COLS] for i in range(3))
    bowl = square - middle * flat

    def down(weights, values):
        a, b, c = (product(weights, part) for part in three_parts(values))
        return a + b + c

    bowl_x = down(along[0], bowl)
    bowl_y = down(along[2], flat) - middle * down(along[0], flat)
    twist = down(along[1], slope)

    taps_at = lax.broadcasted_iota(jnp.int32, (8, COLS), 1) - MAXH
    inside = jnp.abs(taps_at) <= half
    squares = (taps_at * taps_at).astype(jnp.float32)
    width = half.astype(jnp.float32)
    slope_norm = jnp.sum(jnp.where(inside, squares, 0.0), axis=1, keepdims=True)[0:1]
    bowls = squares - middle
    bowl_norm = jnp.sum(jnp.where(inside, bowls * bowls, 0.0), axis=1, keepdims=True)[0:1]
    bowl_scale = 2.0 * width * width / ((2.0 * width + 1.0) * bowl_norm)
    twist_scale = width * width / (slope_norm * slope_norm)
    out[0] = bowl_x * bowl_scale
    out[1] = bowl_y * bowl_scale
    out[2] = twist * twist_scale


def curvature_of(window, rate, sides, above, below):
    return pl.pallas_call(
        curve_kernel,
        out_shape=jax.ShapeDtypeStruct((3, ROWS, COLS), jnp.float32),
        in_specs=[SMEM, VMEM, VMEM, VMEM, VMEM],
        out_specs=VMEM,
        compiler_params=LIMIT,
        name="curve",
    )(window, rate, sides, above, below)


def neighbour(values, axis, count, step):
    return lax.ppermute(values, axis, [(i, i + step) for i in range(count) if 0 <= i + step < count])


def per_device(anomaly, mask, epoch_weight, days, window):
    tau = (days.astype(jnp.float32) - 1826.5) / 365.25
    got = [shift(pack(step, epoch_weight, anomaly, mask), step, True) for step in STEPS]
    early = early_sums(epoch_weight, tau, anomaly, mask, got[0])
    mine = [late_sums(step, tau, early, got[1], got[2]) for step in STEPS + (0,)]
    rest = [shift(total, step, False) for step, total in zip(STEPS, mine)]
    rate, head, tail = fitted_rate(mine[3], rest)
    before = neighbour(tail, "epoch", SIDE * SIDE, 1)
    after = neighbour(head, "epoch", SIDE * SIDE, -1)
    sides, top, bottom = with_sides(rate, before, after)
    above = neighbour(bottom, "tile", TILES, 1)
    below = neighbour(top, "tile", TILES, -1)
    return rate, curvature_of(window, rate, sides, above, below)


def solution(mesh):
    in_specs = (P("epoch", "tile", None), P("epoch", "tile", None), P(), P(), P("tile", "epoch"))
    out_specs = (P("tile", "epoch"), P(None, "tile", "epoch"))
    return jax.shard_map(
        per_device, mesh=mesh, in_specs=in_specs, out_specs=out_specs, check_vma=False
    )
```

```python
import functools

import jax
import jax.numpy as jnp
from jax import lax
from jax.experimental import pallas as pl
from jax.experimental.pallas import tpu as pltpu
from jax.sharding import PartitionSpec as P

MAXH = 16
SIDE = 4
OWN = 4
ROWS = 96
COLS = 128
TILES = 32
AXES = ("epoch", "tile")
STEPS = (2, 1, -1)
ANY = pl.BlockSpec(memory_space=pl.ANY)
SMEM = pl.BlockSpec(memory_space=pltpu.SMEM)
VMEM = pl.BlockSpec(memory_space=pltpu.VMEM)
LIMIT = pltpu.CompilerParams(vmem_limit_bytes=12 << 20)
FIRST_LIMIT = pltpu.CompilerParams(vmem_limit_bytes=62 << 20)
STRIP = 16
BLOCKS = SIDE * SIDE
BESIDE = 2 * MAXH
SLOTS = SIDE + 1
TALL = 6 * ROWS + ROWS // SIDE


def ring_pairs(step, first):
    pairs = []
    for x in range(SIDE):
        for y in range(SIDE):
            for tile in range(TILES):
                if (tile % 2 == 0) == first:
                    there = (x + step) % SIDE * SIDE + y
                else:
                    there = x * SIDE + (y + step) % SIDE
                pairs.append(((x * SIDE + y) * TILES + tile, there * TILES + tile))
    return pairs


def shift(values, step, first):
    return lax.ppermute(values, AXES, ring_pairs(step, first))


def place():
    spot = lax.axis_index("epoch")
    even = lax.axis_index("tile") % 2 == 0
    x, y = spot // SIDE, spot % SIDE
    return jnp.where(even, x, y), jnp.where(even, y, x), even


def block_of(even, first, second):
    return jnp.where(even, SIDE * first + second, SIDE * second + first)


def epoch_of(even, first, second):
    return block_of(even, first, second) * OWN


def columns(block):
    return pl.ds(pl.multiple_of(block * COLS, COLS), COLS)


def lane(shape):
    return lax.broadcasted_iota(jnp.int32, shape, 1)


def group_of(shape):
    return (lane(shape) + MAXH) % COLS // BESIDE


def pack_epoch(step, own, quality, anomaly, mask, out):
    first, second, even = place()
    there = (first + step + SIDE) % SIDE
    weight = quality[epoch_of(even, first, second) + own]
    shape = (ROWS, COLS)
    ahead = lane(shape) < COLS // 2
    group = group_of(shape)
    levels = jnp.zeros(shape, jnp.bfloat16)
    heavies = jnp.zeros(shape, jnp.bfloat16)
    for slot in range(SIDE):
        block = block_of(even, there, slot)
        cols = columns(block)
        before, after = columns(jnp.maximum(block - 1, 0)), columns(jnp.minimum(block + 1, BLOCKS - 1))
        out[slot, own] = anomaly[own, :, cols]
        out[slot, OWN + own] = (mask[own, :, cols].astype(jnp.float32) * weight).astype(jnp.bfloat16)
        level = jnp.where(ahead, anomaly[own, :, after], anomaly[own, :, before])
        valid = jnp.where(ahead, mask[own, :, after], mask[own, :, before]).astype(jnp.float32)
        weights = jnp.where(
            lane((1, COLS)) < COLS // 2,
            jnp.where(block < BLOCKS - 1, weight, 0.0),
            jnp.where(block > 0, weight, 0.0),
        )
        heavy = (valid * weights).astype(jnp.bfloat16)
        if slot:
            level = pltpu.roll(level, slot * BESIDE, 1)
            heavy = pltpu.roll(heavy, slot * BESIDE, 1)
        levels = jnp.where(group == slot, level, levels)
        heavies = jnp.where(group == slot, heavy, heavies)
    out[SIDE, own] = levels
    out[SIDE, OWN + own] = heavies


PACKED = jax.ShapeDtypeStruct((SLOTS, 2 * OWN, ROWS, COLS), jnp.bfloat16)


def read_pack_kernel(steps, quality, anomaly, mask, *refs):
    outs, (level, valid, packed, sems, done) = refs[: len(steps)], refs[len(steps) :]
    copies = []
    for own in range(OWN):
        copies.append(pltpu.make_async_copy(mask.at[own], valid.at[own], sems.at[own, 0]))
        copies.append(pltpu.make_async_copy(anomaly.at[own], level.at[own], sems.at[own, 1]))
    for copy in copies:
        copy.start()
    writes = []
    for own in range(OWN):
        copies[2 * own].wait()
        copies[2 * own + 1].wait()
        for index, (step, out) in enumerate(zip(steps, outs)):
            pack_epoch(step, own, quality, level, valid, packed.at[index])
            for kind, which in enumerate((own, OWN + own)):
                writes.append(
                    pltpu.make_async_copy(packed.at[index, :, which], out.at[:, which], done.at[index, own, kind])
                )
                writes[-1].start()
    for write in writes:
        write.wait()


def read_packs(steps, quality, anomaly, mask):
    width = COLS * BLOCKS
    return pl.pallas_call(
        functools.partial(read_pack_kernel, steps),
        out_shape=(PACKED,) * len(steps),
        in_specs=[SMEM, ANY, ANY],
        out_specs=(ANY,) * len(steps),
        scratch_shapes=[
            pltpu.VMEM((OWN, ROWS, width), jnp.bfloat16),
            pltpu.VMEM((OWN, ROWS, width), jnp.int32),
            pltpu.VMEM((len(steps),) + PACKED.shape, jnp.bfloat16),
            pltpu.SemaphoreType.DMA((OWN, 2)),
            pltpu.SemaphoreType.DMA((len(steps), OWN, 2)),
        ],
        compiler_params=FIRST_LIMIT,
        cost_estimate=pl.CostEstimate(flops=1 << 20, bytes_accessed=5 << 20, transcendentals=0),
        name="read_pack",
    )(quality, anomaly, mask)


def pack_kernel(steps, quality, anomaly, mask, *outs):
    for step, out in zip(steps, outs):
        for own in range(OWN):
            pack_epoch(step, own, quality, anomaly, mask, out)


def packs(steps, quality, anomaly, mask):
    return pl.pallas_call(
        functools.partial(pack_kernel, steps),
        out_shape=(PACKED,) * len(steps),
        in_specs=[SMEM, VMEM, VMEM],
        out_specs=(VMEM,) * len(steps),
        compiler_params=LIMIT,
        cost_estimate=pl.CostEstimate(flops=1 << 20, bytes_accessed=3 << 20, transcendentals=0),
        name="pack",
    )(quality, anomaly, mask)


def added(totals, heavy, height, moment):
    timed = heavy * moment
    loaded = heavy * height
    terms = (heavy, timed, timed * moment, loaded, loaded * moment)
    return terms if totals is None else tuple(map(jnp.add, totals, terms))


def moments_of(tau, moved):
    first, second, even = place()
    base = epoch_of(even, (first - moved + SIDE) % SIDE, second)
    return [tau[base + own] for own in range(OWN)]


def more(totals, packed, slot, at, moments):
    for own in range(OWN):
        heavy = packed[slot, OWN + own, at].astype(jnp.float32)
        totals = added(totals, heavy, packed[slot, own, at].astype(jnp.float32), moments[own])
    return totals


def over_rows(body):
    for index in range(ROWS // STRIP):
        body(pl.ds(index * STRIP, STRIP))


def early_kernel(tau, own, got, out):
    near, far = moments_of(tau, 0), moments_of(tau, STEPS[0])
    for slot in range(SLOTS):

        def body(at):
            totals = more(more(None, own, slot, at, near), got, slot, at, far)
            for which, total in enumerate(totals):
                out[slot, which, at] = total

        over_rows(body)


def early_sums(tau, own, got):
    return pl.pallas_call(
        early_kernel,
        out_shape=jax.ShapeDtypeStruct((SLOTS, 5, ROWS, COLS), jnp.float32),
        in_specs=[SMEM, VMEM, VMEM],
        out_specs=VMEM,
        compiler_params=LIMIT,
        cost_estimate=pl.CostEstimate(flops=1 << 23, bytes_accessed=3 << 20, transcendentals=0),
        name="early",
    )(tau, own, got)


def beside_at(which):
    return pl.ds(which * ROWS, ROWS)


def late_kernel(tau, early, got_b, got_c, out, beside):
    moments = [moments_of(tau, moved) for moved in STEPS[1:]]

    def total_of(slot, at):
        totals = tuple(early[slot, which, at] for which in range(5))
        for got, moment in zip((got_b, got_c), moments):
            totals = more(totals, got, slot, at, moment)
        return totals

    for slot in range(SLOTS):

        def body(at):
            for which, total in enumerate(total_of(slot, at)):
                if slot < SIDE:
                    out[slot, pl.ds(which * ROWS + at.start, STRIP)] = total
                else:
                    beside[which, at] = total

        over_rows(body)
    quarter = ROWS // SIDE
    group = group_of((ROWS, COLS))
    short = group_of((quarter, COLS))

    def turned(values, count):
        return pltpu.roll(values, count % SIDE * BESIDE, 1) if count % SIDE else values

    for slot in range(SIDE):
        full = jnp.zeros((ROWS, COLS), jnp.float32)
        part = jnp.zeros((quarter, COLS), jnp.float32)
        for which in range(SIDE):
            full = jnp.where(group == which, turned(beside[which], which - slot), full)
            piece = beside[4, pl.ds(which * quarter, quarter)]
            part = jnp.where(short == which, turned(piece, which - slot), part)
        out[slot, pl.ds(5 * ROWS, ROWS)] = full
        out[slot, pl.ds(6 * ROWS, quarter)] = part


def late_sums(tau, early, got_b, got_c):
    return pl.pallas_call(
        late_kernel,
        out_shape=jax.ShapeDtypeStruct((SIDE, TALL, COLS), jnp.float32),
        in_specs=[SMEM, VMEM, VMEM, VMEM],
        out_specs=VMEM,
        scratch_shapes=[pltpu.VMEM((5, ROWS, COLS), jnp.float32)],
        compiler_params=LIMIT,
        cost_estimate=pl.CostEstimate(flops=1 << 23, bytes_accessed=4 << 20, transcendentals=0),
        name="late",
    )(tau, early, got_b, got_c)


def second_rings():
    rings = []
    for tile in range(TILES):
        for fixed in range(SIDE):
            spots = [fixed * SIDE + i if tile % 2 == 0 else i * SIDE + fixed for i in range(SIDE)]
            rings.append([spot * TILES + tile for spot in spots])
    return rings


def slope_from(sums):
    lifted = sums[0] + 1.0
    return (lifted * sums[4] - sums[1] * sums[3]) / (lifted * (sums[2] + 1.0) - sums[1] * sums[1])


def rate_kernel(got, rate, again, sides, top, bottom):
    total = got[0] + got[1] + got[2] + got[3]
    value = slope_from([total[which * ROWS : (which + 1) * ROWS] for which in range(5)])
    full = total[5 * ROWS : 6 * ROWS]
    part = total[6 * ROWS :]

    def back(values, which):
        return pltpu.roll(values, COLS - which * BESIDE, 1) if which else values

    spread = [back(full, which) for which in range(4)]
    spread.append(jnp.concatenate([back(part, which) for which in range(SIDE)], axis=0))
    beside = jnp.where(group_of((ROWS, COLS)) == 0, slope_from(spread), 0.0)
    rate[...] = value
    again[...] = value
    sides[...] = beside
    top[...] = jnp.concatenate([value[:MAXH], beside[:MAXH]], axis=0)
    bottom[...] = jnp.concatenate([value[ROWS - MAXH :], beside[ROWS - MAXH :]], axis=0)


def fitted_rate(got):
    block = jax.ShapeDtypeStruct((ROWS, COLS), jnp.float32)
    edge = jax.ShapeDtypeStruct((2 * MAXH, COLS), jnp.float32)
    return pl.pallas_call(
        rate_kernel,
        out_shape=(block, block, block, edge, edge),
        in_specs=[VMEM],
        out_specs=(VMEM,) * 5,
        compiler_params=LIMIT,
        name="rate",
    )(got)


def three_parts(values):
    high = values.astype(jnp.bfloat16)
    rest = values - high.astype(jnp.float32)
    middle = rest.astype(jnp.bfloat16)
    low = (rest - middle.astype(jnp.float32)).astype(jnp.bfloat16)
    return high, middle, low


def taps(offset, half):
    inside = jnp.abs(offset) <= half
    flat = jnp.where(inside, 1.0, 0.0)
    slope = jnp.where(inside, offset, 0).astype(jnp.float32)
    return tuple(v.astype(jnp.bfloat16) for v in (flat, slope, slope * slope))


def product(left, right):
    return jnp.dot(left, right, preferred_element_type=jnp.float32)


def curve_kernel(window, rate, sides, above, below, out):
    half = window[0, 0]
    middle = (half * (half + 1)).astype(jnp.float32) / 3.0
    line = lax.broadcasted_iota(jnp.int32, (2 * COLS, COLS), 0)
    column = jnp.where(line < COLS + MAXH, line, jnp.where(line >= 2 * COLS - MAXH, line - 2 * COLS, 4 * COLS))
    across = jnp.concatenate(taps(column - lane((2 * COLS, COLS)), half), axis=1)
    tall = ROWS + 2 * MAXH
    spot = lane((ROWS, tall))
    row = jnp.where(spot < ROWS, spot, jnp.where(spot < ROWS + MAXH, spot - ROWS - MAXH, spot - MAXH))
    along = taps(row - lax.broadcasted_iota(jnp.int32, (ROWS, tall), 0), half)

    tile = lax.axis_index("tile")
    from_above = jnp.where(tile > 0, above[...], 0.0)
    from_below = jnp.where(tile < TILES - 1, below[...], 0.0)
    main = jnp.concatenate([rate[...], from_above[:MAXH], from_below[:MAXH]], axis=0)
    beside = jnp.concatenate([sides[...], from_above[MAXH:], from_below[MAXH:]], axis=0)
    parts = three_parts(jnp.concatenate([main, beside], axis=1))
    wide = product(parts[0], across) + product(parts[1], across) + product(parts[2], across)
    flat, slope, square = (wide[:, i * COLS : (i + 1) * COLS] for i in range(3))
    bowl = square - middle * flat

    def down(weights, values):
        a, b, c = (product(weights, part) for part in three_parts(values))
        return a + b + c

    bowl_x = down(along[0], bowl)
    bowl_y = down(along[2], flat) - middle * down(along[0], flat)
    twist = down(along[1], slope)

    taps_at = lax.broadcasted_iota(jnp.int32, (8, COLS), 1) - MAXH
    inside = jnp.abs(taps_at) <= half
    squares = (taps_at * taps_at).astype(jnp.float32)
    width = half.astype(jnp.float32)
    slope_norm = jnp.sum(jnp.where(inside, squares, 0.0), axis=1, keepdims=True)[0:1]
    bowls = squares - middle
    bowl_norm = jnp.sum(jnp.where(inside, bowls * bowls, 0.0), axis=1, keepdims=True)[0:1]
    bowl_scale = 2.0 * width * width / ((2.0 * width + 1.0) * bowl_norm)
    twist_scale = width * width / (slope_norm * slope_norm)
    out[0] = bowl_x * bowl_scale
    out[1] = bowl_y * bowl_scale
    out[2] = twist * twist_scale


def curvature_of(window, rate, sides, above, below):
    return pl.pallas_call(
        curve_kernel,
        out_shape=jax.ShapeDtypeStruct((3, ROWS, COLS), jnp.float32),
        in_specs=[SMEM, VMEM, VMEM, VMEM, VMEM],
        out_specs=VMEM,
        compiler_params=LIMIT,
        name="curve",
    )(window, rate, sides, above, below)


def per_device(anomaly, mask, epoch_weight, days, window):
    tau = (days.astype(jnp.float32) - 1826.5) / 365.25
    packed = read_packs(STEPS[:1], epoch_weight, anomaly, mask)
    packed += read_packs(STEPS[1:], epoch_weight, anomaly, mask)
    packed += packs((0,), epoch_weight, anomaly, mask)
    got = [shift(values, step, True) for step, values in zip(STEPS, packed)]
    early = early_sums(tau, packed[3], got[0])
    mine = late_sums(tau, early, got[1], got[2])
    rest = lax.all_to_all(mine, AXES, split_axis=0, concat_axis=0, tiled=True, axis_index_groups=second_rings())
    rate, again, sides, top, bottom = fitted_rate(rest)
    above = lax.ppermute(bottom, "tile", [(i, (i + 1) % TILES) for i in range(TILES)])
    below = lax.ppermute(top, "tile", [(i, (i - 1) % TILES) for i in range(TILES)])
    return rate, curvature_of(window, again, sides, above, below)


def solution(mesh):
    in_specs = (P("epoch", "tile", None), P("epoch", "tile", None), P(), P(), P("tile", "epoch"))
    out_specs = (P("tile", "epoch"), P(None, "tile", "epoch"))
    return jax.shard_map(
        per_device, mesh=mesh, in_specs=in_specs, out_specs=out_specs, check_vma=False
    )
```

```python
import functools

import jax
import jax.numpy as jnp
from jax import lax
from jax.experimental import pallas as pl
from jax.experimental.pallas import tpu as pltpu
from jax.sharding import PartitionSpec as P

MAXH = 16
SIDE = 4
OWN = 4
ROWS = 96
COLS = 128
TILES = 32
AXES = ("epoch", "tile")
STEPS = (2, 1, -1)
ANY = pl.BlockSpec(memory_space=pl.ANY)
SMEM = pl.BlockSpec(memory_space=pltpu.SMEM)
VMEM = pl.BlockSpec(memory_space=pltpu.VMEM)
LIMIT = pltpu.CompilerParams(vmem_limit_bytes=12 << 20)
FIRST_LIMIT = pltpu.CompilerParams(vmem_limit_bytes=62 << 20)
STRIP = 16
BLOCKS = SIDE * SIDE
BESIDE = 2 * MAXH
SLOTS = SIDE + 1
TALL = 6 * ROWS + ROWS // SIDE


def ring_pairs(step, first):
    pairs = []
    for x in range(SIDE):
        for y in range(SIDE):
            for tile in range(TILES):
                if (tile % 2 == 0) == first:
                    there = (x + step) % SIDE * SIDE + y
                else:
                    there = x * SIDE + (y + step) % SIDE
                pairs.append(((x * SIDE + y) * TILES + tile, there * TILES + tile))
    return pairs


def shift(values, step, first):
    return lax.ppermute(values, AXES, ring_pairs(step, first))


def place():
    spot = lax.axis_index("epoch")
    even = lax.axis_index("tile") % 2 == 0
    x, y = spot // SIDE, spot % SIDE
    return jnp.where(even, x, y), jnp.where(even, y, x), even


def block_of(even, first, second):
    return jnp.where(even, SIDE * first + second, SIDE * second + first)


def epoch_of(even, first, second):
    return block_of(even, first, second) * OWN


def columns(block):
    return pl.ds(pl.multiple_of(block * COLS, COLS), COLS)


def lane(shape):
    return lax.broadcasted_iota(jnp.int32, shape, 1)


def group_of(shape):
    return (lane(shape) + MAXH) % COLS // BESIDE


def pack_epoch(step, own, quality, anomaly, mask, out):
    first, second, even = place()
    there = (first + step + SIDE) % SIDE
    weight = quality[epoch_of(even, first, second) + own]
    shape = (ROWS, COLS)
    ahead = lane(shape) < COLS // 2
    group = group_of(shape)
    levels = jnp.zeros(shape, jnp.bfloat16)
    heavies = jnp.zeros(shape, jnp.bfloat16)
    for slot in range(SIDE):
        block = block_of(even, there, slot)
        cols = columns(block)
        before, after = columns(jnp.maximum(block - 1, 0)), columns(jnp.minimum(block + 1, BLOCKS - 1))
        out[slot, own] = anomaly[own, :, cols]
        out[slot, OWN + own] = (mask[own, :, cols].astype(jnp.float32) * weight).astype(jnp.bfloat16)
        level = jnp.where(ahead, anomaly[own, :, after], anomaly[own, :, before])
        valid = jnp.where(ahead, mask[own, :, after], mask[own, :, before]).astype(jnp.float32)
        weights = jnp.where(
            lane((1, COLS)) < COLS // 2,
            jnp.where(block < BLOCKS - 1, weight, 0.0),
            jnp.where(block > 0, weight, 0.0),
        )
        heavy = (valid * weights).astype(jnp.bfloat16)
        if slot:
            level = pltpu.roll(level, slot * BESIDE, 1)
            heavy = pltpu.roll(heavy, slot * BESIDE, 1)
        levels = jnp.where(group == slot, level, levels)
        heavies = jnp.where(group == slot, heavy, heavies)
    out[SIDE, own] = levels
    out[SIDE, OWN + own] = heavies


PACKED = jax.ShapeDtypeStruct((SLOTS, 2 * OWN, ROWS, COLS), jnp.bfloat16)


def read_windows(steps, even, first):
    if len(steps) > 1:
        return (((0, BLOCKS),),) * 2
    there = (first + steps[0] + SIDE) % SIDE
    run = SIDE + 2
    on_even = ((jnp.clip(SIDE * there - 1, 0, BLOCKS - run), run),)
    on_odd = tuple((jnp.clip(SIDE * slot + there - 1, 0, BLOCKS - 3), 3) for slot in range(SIDE))
    return on_even, on_odd


def read_pack_kernel(steps, quality, anomaly, mask, *refs):
    outs, (level, valid, packed, own_quality, sems, done, ready) = refs[: len(steps)], refs[len(steps) :]
    known = pltpu.make_async_copy(quality, own_quality, ready)
    known.start()
    first, second, even = place()
    on_even, on_odd = read_windows(steps, even, first)

    def reads(windows, own):
        for index, (start, blocks) in enumerate(windows):
            cols = pl.ds(pl.multiple_of(start * COLS, COLS), blocks * COLS)
            yield pltpu.make_async_copy(mask.at[own, :, cols], valid.at[own, :, cols], sems.at[own, index, 0])
            yield pltpu.make_async_copy(anomaly.at[own, :, cols], level.at[own, :, cols], sems.at[own, index, 1])

    def on_parity(act):
        if on_even is on_odd:
            act(on_even)
        else:
            pl.when(even)(lambda: act(on_even))
            pl.when(jnp.logical_not(even))(lambda: act(on_odd))

    def start(windows):
        for own in range(OWN):
            for copy in reads(windows, own):
                copy.start()

    on_parity(start)
    known.wait()
    writes = []
    for own in range(OWN):

        def wait(windows):
            for copy in reads(windows, own):
                copy.wait()

        on_parity(wait)
        for index, (step, out) in enumerate(zip(steps, outs)):
            pack_epoch(step, own, own_quality, level, valid, packed.at[index])
            for kind, which in enumerate((own, OWN + own)):
                writes.append(
                    pltpu.make_async_copy(packed.at[index, :, which], out.at[:, which], done.at[index, own, kind])
                )
                writes[-1].start()
    for write in writes:
        write.wait()


def read_packs(steps, quality, anomaly, mask):
    width = COLS * BLOCKS
    return pl.pallas_call(
        functools.partial(read_pack_kernel, steps),
        out_shape=(PACKED,) * len(steps),
        in_specs=[ANY, ANY, ANY],
        out_specs=(ANY,) * len(steps),
        scratch_shapes=[
            pltpu.VMEM((OWN, ROWS, width), jnp.bfloat16),
            pltpu.VMEM((OWN, ROWS, width), jnp.int32),
            pltpu.VMEM((len(steps),) + PACKED.shape, jnp.bfloat16),
            pltpu.SMEM((BLOCKS * OWN,), jnp.float32),
            pltpu.SemaphoreType.DMA((OWN, SIDE, 2)),
            pltpu.SemaphoreType.DMA((len(steps), OWN, 2)),
            pltpu.SemaphoreType.DMA,
        ],
        compiler_params=FIRST_LIMIT,
        cost_estimate=pl.CostEstimate(flops=1 << 20, bytes_accessed=5 << 20, transcendentals=0),
        name="read_pack",
    )(quality, anomaly, mask)


def pack_kernel(steps, quality, anomaly, mask, *outs):
    for step, out in zip(steps, outs):
        for own in range(OWN):
            pack_epoch(step, own, quality, anomaly, mask, out)


def packs(steps, quality, anomaly, mask):
    return pl.pallas_call(
        functools.partial(pack_kernel, steps),
        out_shape=(PACKED,) * len(steps),
        in_specs=[SMEM, VMEM, VMEM],
        out_specs=(VMEM,) * len(steps),
        compiler_params=LIMIT,
        cost_estimate=pl.CostEstimate(flops=1 << 20, bytes_accessed=3 << 20, transcendentals=0),
        name="pack",
    )(quality, anomaly, mask)


def added(totals, heavy, height, moment):
    timed = heavy * moment
    loaded = heavy * height
    terms = (heavy, timed, timed * moment, loaded, loaded * moment)
    return terms if totals is None else tuple(map(jnp.add, totals, terms))


def moments_of(tau, moved):
    first, second, even = place()
    base = epoch_of(even, (first - moved + SIDE) % SIDE, second)
    return [tau[base + own] for own in range(OWN)]


def more(totals, packed, slot, at, moments):
    for own in range(OWN):
        heavy = packed[slot, OWN + own, at].astype(jnp.float32)
        totals = added(totals, heavy, packed[slot, own, at].astype(jnp.float32), moments[own])
    return totals


def over_rows(body):
    for index in range(ROWS // STRIP):
        body(pl.ds(index * STRIP, STRIP))


EDGES = 2 * MAXH
TIMES = jax.ShapeDtypeStruct((2, OWN, STRIP, COLS), jnp.float32)
PREPARED = (
    jax.ShapeDtypeStruct((2 * COLS, 3 * COLS), jnp.bfloat16),
    jax.ShapeDtypeStruct((3, ROWS, ROWS), jnp.bfloat16),
    jax.ShapeDtypeStruct((3, EDGES, EDGES), jnp.bfloat16),
    jax.ShapeDtypeStruct((3, 8, COLS), jnp.float32),
)


def taps(offset, half):
    inside = jnp.abs(offset) <= half
    flat = jnp.where(inside, 1.0, 0.0)
    slope = jnp.where(inside, offset, 0).astype(jnp.float32)
    return tuple(v.astype(jnp.bfloat16) for v in (flat, slope, slope * slope))


def prepare(half, across, along, beyond, factors):
    line = lax.broadcasted_iota(jnp.int32, (2 * COLS, COLS), 0)
    column = jnp.where(line < COLS + MAXH, line, jnp.where(line >= 2 * COLS - MAXH, line - 2 * COLS, 4 * COLS))
    across[...] = jnp.concatenate(taps(column - lane((2 * COLS, COLS)), half), axis=1)
    shape = (ROWS, ROWS)
    for which, tap in enumerate(taps(lane(shape) - lax.broadcasted_iota(jnp.int32, shape, 0), half)):
        along[which] = tap
    shape = (EDGES, EDGES)
    spot = lane(shape)
    mine = lax.broadcasted_iota(jnp.int32, shape, 0)
    row = jnp.where(spot < MAXH, spot - MAXH, spot + ROWS - MAXH)
    mine = jnp.where(mine < MAXH, mine, mine + ROWS - EDGES)
    for which, tap in enumerate(taps(row - mine, half)):
        beyond[which] = tap
    middle = (half * (half + 1)).astype(jnp.float32) / 3.0
    width = half.astype(jnp.float32)
    taps_at = lane((8, COLS)) - MAXH
    inside = jnp.abs(taps_at) <= half
    squares = (taps_at * taps_at).astype(jnp.float32)
    bowls = squares - middle
    slope_norm = jnp.sum(jnp.where(inside, squares, 0.0), axis=1, keepdims=True)
    bowl_norm = jnp.sum(jnp.where(inside, bowls * bowls, 0.0), axis=1, keepdims=True)
    shape = (8, COLS)
    factors[0] = jnp.full(shape, middle, jnp.float32)
    factors[1] = jnp.broadcast_to(2.0 * width * width / ((2.0 * width + 1.0) * bowl_norm), shape)
    factors[2] = jnp.broadcast_to(width * width / (slope_norm * slope_norm), shape)


def early_kernel(tau, window, own, got, out, times, *prepared):
    near, far = moments_of(tau, 0), moments_of(tau, STEPS[0])
    for index, moved in enumerate(STEPS[1:]):
        for which, moment in enumerate(moments_of(tau, moved)):
            times[index, which] = jnp.full((STRIP, COLS), moment, jnp.float32)
    for slot in range(SLOTS):

        def body(at):
            totals = more(more(None, own, slot, at, near), got, slot, at, far)
            for which, total in enumerate(totals):
                out[slot, which, at] = total

        over_rows(body)
    prepare(window[0, 0], *prepared)


def early_sums(tau, window, own, got):
    return pl.pallas_call(
        early_kernel,
        out_shape=(jax.ShapeDtypeStruct((SLOTS, 5, ROWS, COLS), jnp.float32), TIMES) + PREPARED,
        in_specs=[SMEM, SMEM, VMEM, VMEM],
        out_specs=(VMEM,) * 6,
        compiler_params=LIMIT,
        cost_estimate=pl.CostEstimate(flops=1 << 23, bytes_accessed=3 << 20, transcendentals=0),
        name="early",
    )(tau, window, own, got)


def late_kernel(times, early, got_b, got_c, out, beside):
    moments = [[times[index, own] for own in range(OWN)] for index in range(2)]

    def total_of(slot, at):
        totals = tuple(early[slot, which, at] for which in range(5))
        for got, moment in zip((got_b, got_c), moments):
            totals = more(totals, got, slot, at, moment)
        return totals

    for slot in range(SLOTS):

        def body(at):
            for which, total in enumerate(total_of(slot, at)):
                if slot < SIDE:
                    out[slot, pl.ds(which * ROWS + at.start, STRIP)] = total
                else:
                    beside[which, at] = total

        over_rows(body)
    quarter = ROWS // SIDE
    group = group_of((ROWS, COLS))
    short = group_of((quarter, COLS))

    def turned(values, count):
        return pltpu.roll(values, count % SIDE * BESIDE, 1) if count % SIDE else values

    for slot in range(SIDE):
        full = jnp.zeros((ROWS, COLS), jnp.float32)
        part = jnp.zeros((quarter, COLS), jnp.float32)
        for which in range(SIDE):
            full = jnp.where(group == which, turned(beside[which], which - slot), full)
            piece = beside[4, pl.ds(which * quarter, quarter)]
            part = jnp.where(short == which, turned(piece, which - slot), part)
        out[slot, pl.ds(5 * ROWS, ROWS)] = full
        out[slot, pl.ds(6 * ROWS, quarter)] = part


def late_sums(times, early, got_b, got_c):
    return pl.pallas_call(
        late_kernel,
        out_shape=jax.ShapeDtypeStruct((SIDE, TALL, COLS), jnp.float32),
        in_specs=[VMEM, VMEM, VMEM, VMEM],
        out_specs=VMEM,
        scratch_shapes=[pltpu.VMEM((5, ROWS, COLS), jnp.float32)],
        compiler_params=LIMIT,
        cost_estimate=pl.CostEstimate(flops=1 << 23, bytes_accessed=4 << 20, transcendentals=0),
        name="late",
    )(times, early, got_b, got_c)


def second_rings():
    rings = []
    for tile in range(TILES):
        for fixed in range(SIDE):
            spots = [fixed * SIDE + i if tile % 2 == 0 else i * SIDE + fixed for i in range(SIDE)]
            rings.append([spot * TILES + tile for spot in spots])
    return rings


def slope_from(sums):
    lifted = sums[0] + 1.0
    return (lifted * sums[4] - sums[1] * sums[3]) / (lifted * (sums[2] + 1.0) - sums[1] * sums[1])


def rate_kernel(got, rate, sides, top, bottom):
    total = got[0] + got[1] + got[2] + got[3]
    value = slope_from([total[which * ROWS : (which + 1) * ROWS] for which in range(5)])
    full = total[5 * ROWS : 6 * ROWS]
    part = total[6 * ROWS :]

    def back(values, which):
        return pltpu.roll(values, COLS - which * BESIDE, 1) if which else values

    spread = [back(full, which) for which in range(4)]
    spread.append(jnp.concatenate([back(part, which) for which in range(SIDE)], axis=0))
    beside = jnp.where(group_of((ROWS, COLS)) == 0, slope_from(spread), 0.0)
    rate[...] = value
    sides[...] = beside
    top[...] = jnp.concatenate([value[:MAXH], beside[:MAXH]], axis=0)
    bottom[...] = jnp.concatenate([value[ROWS - MAXH :], beside[ROWS - MAXH :]], axis=0)


def fitted_rate(got):
    block = jax.ShapeDtypeStruct((ROWS, COLS), jnp.float32)
    edge = jax.ShapeDtypeStruct((2 * MAXH, COLS), jnp.float32)
    return pl.pallas_call(
        rate_kernel,
        out_shape=(block, block, edge, edge),
        in_specs=[VMEM],
        out_specs=(VMEM,) * 4,
        compiler_params=LIMIT,
        name="rate",
    )(got)


def three_parts(values):
    high = values.astype(jnp.bfloat16)
    rest = values - high.astype(jnp.float32)
    middle = rest.astype(jnp.bfloat16)
    low = (rest - middle.astype(jnp.float32)).astype(jnp.bfloat16)
    return high, middle, low


def product(left, right):
    return jnp.dot(left, right, preferred_element_type=jnp.float32)


def over_columns(values, across, middle):
    parts = three_parts(values)
    wide = product(parts[0], across) + product(parts[1], across) + product(parts[2], across)
    flat, slope, square = (wide[:, i * COLS : (i + 1) * COLS] for i in range(3))
    return flat, slope, square - middle * flat


def over_lines(along, sums, middle):
    flat, slope, bowl = sums

    def down(weights, values):
        a, b, c = (product(weights, part) for part in three_parts(values))
        return a + b + c

    return down(along[0], bowl), down(along[2], flat) - middle * down(along[0], flat), down(along[1], slope)


SCALE_OF = (1, 1, 2)
INNER = ROWS - EDGES


def within_kernel(fitted, sides, across, along, factors, inner, partial):
    middle = factors[0, 0:1]
    sums = over_columns(jnp.concatenate([fitted[...], sides[...]], axis=1), across[...], middle)
    for which, value in enumerate(over_lines(along, sums, middle)):
        inner[which] = value[MAXH : ROWS - MAXH] * factors[SCALE_OF[which], 0:1]
        partial[which] = jnp.concatenate([value[:MAXH], value[ROWS - MAXH :]], axis=0)


def within(fitted, sides, across, along, factors):
    return pl.pallas_call(
        within_kernel,
        out_shape=(
            jax.ShapeDtypeStruct((3, INNER, COLS), jnp.float32),
            jax.ShapeDtypeStruct((3, EDGES, COLS), jnp.float32),
        ),
        in_specs=[VMEM] * 5,
        out_specs=(VMEM, VMEM),
        compiler_params=LIMIT,
        cost_estimate=pl.CostEstimate(flops=1 << 27, bytes_accessed=1 << 20, transcendentals=0),
        name="within",
    )(fitted, sides, across, along, factors)


def finish_kernel(across, beyond, factors, fitted, inner, partial, above, below, rate, out, edge, sems):
    writes = [
        pltpu.make_async_copy(fitted, rate, sems.at[0]),
        pltpu.make_async_copy(inner, out.at[:, pl.ds(MAXH, INNER)], sems.at[1]),
        pltpu.make_async_copy(edge.at[:, pl.ds(0, MAXH)], out.at[:, pl.ds(0, MAXH)], sems.at[2]),
        pltpu.make_async_copy(edge.at[:, pl.ds(MAXH, MAXH)], out.at[:, pl.ds(ROWS - MAXH, MAXH)], sems.at[3]),
    ]
    for write in writes[:2]:
        write.start()
    middle = factors[0, 0:1]
    tile = lax.axis_index("tile")
    up = jnp.where(tile > 0, above[...], 0.0)
    down = jnp.where(tile < TILES - 1, below[...], 0.0)
    values = [jnp.concatenate([part[:MAXH], part[MAXH:]], axis=1) for part in (up, down)]
    sums = over_columns(jnp.concatenate(values, axis=0), across[...], middle)
    for which, value in enumerate(over_lines(beyond, sums, middle)):
        edge[which] = (partial[which] + value) * factors[SCALE_OF[which], 0:1]
    for write in writes[2:]:
        write.start()
    for write in writes:
        write.wait()


def finish(across, beyond, factors, fitted, inner, partial, above, below):
    return pl.pallas_call(
        finish_kernel,
        out_shape=(
            jax.ShapeDtypeStruct((ROWS, COLS), jnp.float32),
            jax.ShapeDtypeStruct((3, ROWS, COLS), jnp.float32),
        ),
        in_specs=[VMEM] * 8,
        out_specs=(ANY, ANY),
        scratch_shapes=[pltpu.VMEM((3, EDGES, COLS), jnp.float32), pltpu.SemaphoreType.DMA((4,))],
        compiler_params=LIMIT,
        name="finish",
    )(across, beyond, factors, fitted, inner, partial, above, below)


def per_device(anomaly, mask, epoch_weight, days, window):
    tau = (days.astype(jnp.float32) - 1826.5) / 365.25
    packed = read_packs(STEPS[:1], epoch_weight, anomaly, mask)
    packed += read_packs(STEPS[1:], epoch_weight, anomaly, mask)
    packed += packs((0,), epoch_weight, anomaly, mask)
    got = [shift(values, step, True) for step, values in zip(STEPS, packed)]
    early, times, across, along, beyond, factors = early_sums(tau, window, packed[3], got[0])
    mine = late_sums(times, early, got[1], got[2])
    rest = lax.all_to_all(mine, AXES, split_axis=0, concat_axis=0, tiled=True, axis_index_groups=second_rings())
    fitted, sides, top, bottom = fitted_rate(rest)
    above = lax.ppermute(bottom, "tile", [(i, (i + 1) % TILES) for i in range(TILES)])
    below = lax.ppermute(top, "tile", [(i, (i - 1) % TILES) for i in range(TILES)])
    inner, partial = within(fitted, sides, across, along, factors)
    return finish(across, beyond, factors, fitted, inner, partial, above, below)


def solution(mesh):
    in_specs = (P("epoch", "tile", None), P("epoch", "tile", None), P(), P(), P("tile", "epoch"))
    out_specs = (P("tile", "epoch"), P(None, "tile", "epoch"))
    return jax.shard_map(
        per_device, mesh=mesh, in_specs=in_specs, out_specs=out_specs, check_vma=False
    )
```

```python
import functools

import jax
import jax.numpy as jnp
from jax import lax
from jax.experimental import pallas as pl
from jax.experimental.pallas import tpu as pltpu
from jax.sharding import PartitionSpec as P

MAXH = 16
SIDE = 4
OWN = 4
ROWS = 96
COLS = 128
TILES = 32
AXES = ("epoch", "tile")
STEPS = (2, 1, -1)
ANY = pl.BlockSpec(memory_space=pl.ANY)
SMEM = pl.BlockSpec(memory_space=pltpu.SMEM)
VMEM = pl.BlockSpec(memory_space=pltpu.VMEM)
LIMIT = pltpu.CompilerParams(vmem_limit_bytes=12 << 20)
FIRST_LIMIT = pltpu.CompilerParams(vmem_limit_bytes=62 << 20)
STRIP = 16
BLOCKS = SIDE * SIDE
BESIDE = 2 * MAXH
SLOTS = SIDE + 1
TALL = 6 * ROWS + ROWS // SIDE


def ring_pairs(step, first):
    pairs = []
    for x in range(SIDE):
        for y in range(SIDE):
            for tile in range(TILES):
                if (tile % 2 == 0) == first:
                    there = (x + step) % SIDE * SIDE + y
                else:
                    there = x * SIDE + (y + step) % SIDE
                pairs.append(((x * SIDE + y) * TILES + tile, there * TILES + tile))
    return pairs


def shift(values, step, first):
    return lax.ppermute(values, AXES, ring_pairs(step, first))


def place():
    spot = lax.axis_index("epoch")
    even = lax.axis_index("tile") % 2 == 0
    x, y = spot // SIDE, spot % SIDE
    return jnp.where(even, x, y), jnp.where(even, y, x), even


def block_of(even, first, second):
    return jnp.where(even, SIDE * first + second, SIDE * second + first)


def epoch_of(even, first, second):
    return block_of(even, first, second) * OWN


def columns(block):
    return pl.ds(pl.multiple_of(block * COLS, COLS), COLS)


def lane(shape):
    return lax.broadcasted_iota(jnp.int32, shape, 1)


def group_of(shape):
    return (lane(shape) + MAXH) % COLS // BESIDE


def pack_epoch(step, own, quality, anomaly, mask, out):
    first, second, even = place()
    there = (first + step + SIDE) % SIDE
    weight = quality[epoch_of(even, first, second) + own]
    shape = (ROWS, COLS)
    ahead = lane(shape) < COLS // 2
    group = group_of(shape)
    levels = jnp.zeros(shape, jnp.bfloat16)
    heavies = jnp.zeros(shape, jnp.bfloat16)
    for slot in range(SIDE):
        block = block_of(even, there, slot)
        cols = columns(block)
        before, after = columns(jnp.maximum(block - 1, 0)), columns(jnp.minimum(block + 1, BLOCKS - 1))
        out[slot, own] = anomaly[own, :, cols]
        out[slot, OWN + own] = (mask[own, :, cols].astype(jnp.float32) * weight).astype(jnp.bfloat16)
        level = jnp.where(ahead, anomaly[own, :, after], anomaly[own, :, before])
        valid = jnp.where(ahead, mask[own, :, after], mask[own, :, before]).astype(jnp.float32)
        weights = jnp.where(
            lane((1, COLS)) < COLS // 2,
            jnp.where(block < BLOCKS - 1, weight, 0.0),
            jnp.where(block > 0, weight, 0.0),
        )
        heavy = (valid * weights).astype(jnp.bfloat16)
        if slot:
            level = pltpu.roll(level, slot * BESIDE, 1)
            heavy = pltpu.roll(heavy, slot * BESIDE, 1)
        levels = jnp.where(group == slot, level, levels)
        heavies = jnp.where(group == slot, heavy, heavies)
    out[SIDE, own] = levels
    out[SIDE, OWN + own] = heavies


PACKED = jax.ShapeDtypeStruct((SLOTS, 2 * OWN, ROWS, COLS), jnp.bfloat16)


def read_windows(steps, even, first):
    if len(steps) > 1:
        return (((0, BLOCKS),),) * 2
    there = (first + steps[0] + SIDE) % SIDE
    run = SIDE + 2
    on_even = ((jnp.clip(SIDE * there - 1, 0, BLOCKS - run), run),)
    on_odd = tuple((jnp.clip(SIDE * slot + there - 1, 0, BLOCKS - 3), 3) for slot in range(SIDE))
    return on_even, on_odd


def read_pack_kernel(steps, quality, anomaly, mask, *refs):
    outs, (level, valid, packed, own_quality, sems, done, ready) = refs[: len(steps)], refs[len(steps) :]
    known = pltpu.make_async_copy(quality, own_quality, ready)
    known.start()
    first, second, even = place()
    on_even, on_odd = read_windows(steps, even, first)

    def reads(windows, own):
        for index, (start, blocks) in enumerate(windows):
            cols = pl.ds(pl.multiple_of(start * COLS, COLS), blocks * COLS)
            yield pltpu.make_async_copy(mask.at[own, :, cols], valid.at[own, :, cols], sems.at[own, index, 0])
            yield pltpu.make_async_copy(anomaly.at[own, :, cols], level.at[own, :, cols], sems.at[own, index, 1])

    def on_parity(act):
        if on_even is on_odd:
            act(on_even)
        else:
            pl.when(even)(lambda: act(on_even))
            pl.when(jnp.logical_not(even))(lambda: act(on_odd))

    def start(windows):
        for own in range(OWN):
            for copy in reads(windows, own):
                copy.start()

    on_parity(start)
    known.wait()
    writes = []
    for own in range(OWN):

        def wait(windows):
            for copy in reads(windows, own):
                copy.wait()

        on_parity(wait)
        for index, (step, out) in enumerate(zip(steps, outs)):
            pack_epoch(step, own, own_quality, level, valid, packed.at[index])
            for kind, which in enumerate((own, OWN + own)):
                writes.append(
                    pltpu.make_async_copy(packed.at[index, :, which], out.at[:, which], done.at[index, own, kind])
                )
                writes[-1].start()
    for write in writes:
        write.wait()


def read_packs(steps, quality, anomaly, mask):
    width = COLS * BLOCKS
    return pl.pallas_call(
        functools.partial(read_pack_kernel, steps),
        out_shape=(PACKED,) * len(steps),
        in_specs=[ANY, ANY, ANY],
        out_specs=(ANY,) * len(steps),
        scratch_shapes=[
            pltpu.VMEM((OWN, ROWS, width), jnp.bfloat16),
            pltpu.VMEM((OWN, ROWS, width), jnp.int32),
            pltpu.VMEM((len(steps),) + PACKED.shape, jnp.bfloat16),
            pltpu.SMEM((BLOCKS * OWN,), jnp.float32),
            pltpu.SemaphoreType.DMA((OWN, SIDE, 2)),
            pltpu.SemaphoreType.DMA((len(steps), OWN, 2)),
            pltpu.SemaphoreType.DMA,
        ],
        compiler_params=FIRST_LIMIT,
        cost_estimate=pl.CostEstimate(flops=1 << 20, bytes_accessed=5 << 20, transcendentals=0),
        name="read_pack",
    )(quality, anomaly, mask)


def pack_kernel(steps, quality, anomaly, mask, *outs):
    for step, out in zip(steps, outs):
        for own in range(OWN):
            pack_epoch(step, own, quality, anomaly, mask, out)


def packs(steps, quality, anomaly, mask):
    return pl.pallas_call(
        functools.partial(pack_kernel, steps),
        out_shape=(PACKED,) * len(steps),
        in_specs=[SMEM, VMEM, VMEM],
        out_specs=(VMEM,) * len(steps),
        compiler_params=LIMIT,
        cost_estimate=pl.CostEstimate(flops=1 << 20, bytes_accessed=3 << 20, transcendentals=0),
        name="pack",
    )(quality, anomaly, mask)


def added(totals, heavy, height, moment):
    timed = heavy * moment
    loaded = heavy * height
    terms = (heavy, timed, timed * moment, loaded, loaded * moment)
    return terms if totals is None else tuple(map(jnp.add, totals, terms))


def moments_of(tau, moved):
    first, second, even = place()
    base = epoch_of(even, (first - moved + SIDE) % SIDE, second)
    return [tau[base + own] for own in range(OWN)]


def more(totals, packed, slot, at, moments):
    for own in range(OWN):
        heavy = packed[slot, OWN + own, at].astype(jnp.float32)
        totals = added(totals, heavy, packed[slot, own, at].astype(jnp.float32), moments[own])
    return totals


def over_rows(body):
    for index in range(ROWS // STRIP):
        body(pl.ds(index * STRIP, STRIP))


EDGES = 2 * MAXH
TAPS = 4
TIMES = jax.ShapeDtypeStruct((2, OWN, STRIP, COLS), jnp.float32)
PREPARED = (
    jax.ShapeDtypeStruct((2 * COLS, TAPS * COLS), jnp.bfloat16),
    jax.ShapeDtypeStruct((TAPS, ROWS, ROWS), jnp.bfloat16),
    jax.ShapeDtypeStruct((TAPS, EDGES, EDGES), jnp.bfloat16),
    jax.ShapeDtypeStruct((2, 8, COLS), jnp.float32),
)


def bowl_taps(offset, half):
    return (3 * offset * offset - half * (half + 1)).astype(jnp.float32)


def taps(offset, half):
    inside = jnp.abs(offset) <= half
    flat = jnp.where(inside, 1.0, 0.0).astype(jnp.bfloat16)
    slope = jnp.where(inside, offset, 0).astype(jnp.float32).astype(jnp.bfloat16)
    bowl = jnp.where(inside, bowl_taps(offset, half), 0.0)
    most = bowl.astype(jnp.bfloat16)
    return flat, slope, most, (bowl - most.astype(jnp.float32)).astype(jnp.bfloat16)


def prepare(half, across, along, beyond, factors):
    line = lax.broadcasted_iota(jnp.int32, (2 * COLS, COLS), 0)
    column = jnp.where(line < COLS + MAXH, line, jnp.where(line >= 2 * COLS - MAXH, line - 2 * COLS, 4 * COLS))
    across[...] = jnp.concatenate(taps(column - lane((2 * COLS, COLS)), half), axis=1)
    shape = (ROWS, ROWS)
    for which, tap in enumerate(taps(lane(shape) - lax.broadcasted_iota(jnp.int32, shape, 0), half)):
        along[which] = tap
    shape = (EDGES, EDGES)
    spot = lane(shape)
    mine = lax.broadcasted_iota(jnp.int32, shape, 0)
    row = jnp.where(spot < MAXH, spot - MAXH, spot + ROWS - MAXH)
    mine = jnp.where(mine < MAXH, mine, mine + ROWS - EDGES)
    for which, tap in enumerate(taps(row - mine, half)):
        beyond[which] = tap
    width = half.astype(jnp.float32)
    taps_at = lane((8, COLS)) - MAXH
    inside = jnp.abs(taps_at) <= half
    squares = (taps_at * taps_at).astype(jnp.float32)
    bowls = bowl_taps(taps_at, half)
    slope_norm = jnp.sum(jnp.where(inside, squares, 0.0), axis=1, keepdims=True)
    bowl_norm = jnp.sum(jnp.where(inside, bowls * bowls, 0.0), axis=1, keepdims=True)
    shape = (8, COLS)
    factors[0] = jnp.broadcast_to(6.0 * width * width / ((2.0 * width + 1.0) * bowl_norm), shape)
    factors[1] = jnp.broadcast_to(width * width / (slope_norm * slope_norm), shape)


def early_kernel(tau, window, own, got, out, times, *prepared):
    near, far = moments_of(tau, 0), moments_of(tau, STEPS[0])
    for index, moved in enumerate(STEPS[1:]):
        for which, moment in enumerate(moments_of(tau, moved)):
            times[index, which] = jnp.full((STRIP, COLS), moment, jnp.float32)
    for slot in range(SLOTS):

        def body(at):
            totals = more(more(None, own, slot, at, near), got, slot, at, far)
            for which, total in enumerate(totals):
                out[slot, which, at] = total

        over_rows(body)
    prepare(window[0, 0], *prepared)


def early_sums(tau, window, own, got):
    return pl.pallas_call(
        early_kernel,
        out_shape=(jax.ShapeDtypeStruct((SLOTS, 5, ROWS, COLS), jnp.float32), TIMES) + PREPARED,
        in_specs=[SMEM, SMEM, VMEM, VMEM],
        out_specs=(VMEM,) * 6,
        compiler_params=LIMIT,
        cost_estimate=pl.CostEstimate(flops=1 << 23, bytes_accessed=3 << 20, transcendentals=0),
        name="early",
    )(tau, window, own, got)


def late_kernel(times, early, got_b, got_c, out, beside):
    moments = [[times[index, own] for own in range(OWN)] for index in range(2)]

    def total_of(slot, at):
        totals = tuple(early[slot, which, at] for which in range(5))
        for got, moment in zip((got_b, got_c), moments):
            totals = more(totals, got, slot, at, moment)
        return totals

    for slot in (SIDE,) + tuple(range(SIDE)):

        def body(at):
            for which, total in enumerate(total_of(slot, at)):
                if slot < SIDE:
                    out[slot, pl.ds(which * ROWS + at.start, STRIP)] = total
                else:
                    beside[which, at] = total

        over_rows(body)
    quarter = ROWS // SIDE
    group = group_of((ROWS, COLS))
    short = group_of((quarter, COLS))

    def turned(values, count):
        return pltpu.roll(values, count % SIDE * BESIDE, 1) if count % SIDE else values

    for slot in range(SIDE):
        full = jnp.zeros((ROWS, COLS), jnp.float32)
        part = jnp.zeros((quarter, COLS), jnp.float32)
        for which in range(SIDE):
            full = jnp.where(group == which, turned(beside[which], which - slot), full)
            piece = beside[4, pl.ds(which * quarter, quarter)]
            part = jnp.where(short == which, turned(piece, which - slot), part)
        out[slot, pl.ds(5 * ROWS, ROWS)] = full
        out[slot, pl.ds(6 * ROWS, quarter)] = part


def late_sums(times, early, got_b, got_c):
    return pl.pallas_call(
        late_kernel,
        out_shape=jax.ShapeDtypeStruct((SIDE, TALL, COLS), jnp.float32),
        in_specs=[VMEM, VMEM, VMEM, VMEM],
        out_specs=VMEM,
        scratch_shapes=[pltpu.VMEM((5, ROWS, COLS), jnp.float32)],
        compiler_params=LIMIT,
        cost_estimate=pl.CostEstimate(flops=1 << 23, bytes_accessed=4 << 20, transcendentals=0),
        name="late",
    )(times, early, got_b, got_c)


def second_rings():
    rings = []
    for tile in range(TILES):
        for fixed in range(SIDE):
            spots = [fixed * SIDE + i if tile % 2 == 0 else i * SIDE + fixed for i in range(SIDE)]
            rings.append([spot * TILES + tile for spot in spots])
    return rings


def slope_from(sums):
    lifted = sums[0] + 1.0
    return (lifted * sums[4] - sums[1] * sums[3]) / (lifted * (sums[2] + 1.0) - sums[1] * sums[1])


def rate_kernel(got, rate, sides, top, bottom):
    total = got[0] + got[1] + got[2] + got[3]
    value = slope_from([total[which * ROWS : (which + 1) * ROWS] for which in range(5)])
    full = total[5 * ROWS : 6 * ROWS]
    part = total[6 * ROWS :]

    def back(values, which):
        return pltpu.roll(values, COLS - which * BESIDE, 1) if which else values

    spread = [back(full, which) for which in range(4)]
    spread.append(jnp.concatenate([back(part, which) for which in range(SIDE)], axis=0))
    beside = jnp.where(group_of((ROWS, COLS)) == 0, slope_from(spread), 0.0)
    rate[...] = value
    sides[...] = beside
    top[...] = jnp.concatenate([value[:MAXH], beside[:MAXH]], axis=0)
    bottom[...] = jnp.concatenate([value[ROWS - MAXH :], beside[ROWS - MAXH :]], axis=0)


def fitted_rate(got):
    block = jax.ShapeDtypeStruct((ROWS, COLS), jnp.float32)
    edge = jax.ShapeDtypeStruct((2 * MAXH, COLS), jnp.float32)
    return pl.pallas_call(
        rate_kernel,
        out_shape=(block, block, edge, edge),
        in_specs=[VMEM],
        out_specs=(VMEM,) * 4,
        compiler_params=LIMIT,
        name="rate",
    )(got)


def three_parts(values):
    high = values.astype(jnp.bfloat16)
    rest = values - high.astype(jnp.float32)
    middle = rest.astype(jnp.bfloat16)
    low = (rest - middle.astype(jnp.float32)).astype(jnp.bfloat16)
    return high, middle, low


def product(left, right):
    return jnp.dot(left, right, preferred_element_type=jnp.float32)


def over_columns(values, across):
    parts = three_parts(values)
    wide = product(parts[0], across) + product(parts[1], across) + product(parts[2], across)
    flat, slope, most, rest = (wide[:, i * COLS : (i + 1) * COLS] for i in range(TAPS))
    return flat, slope, most + rest


def over_lines(along, sums):
    flat, slope, bowl = sums

    def down(weights, values):
        a, b, c = (product(weights, part) for part in three_parts(values))
        return a + b + c

    return down(along[0], bowl), down(along[2], flat) + down(along[3], flat), down(along[1], slope)


SCALE_OF = (0, 0, 1)
INNER = ROWS - EDGES


def within_kernel(fitted, sides, across, along, factors, inner, partial):
    sums = over_columns(jnp.concatenate([fitted[...], sides[...]], axis=1), across[...])
    for which, value in enumerate(over_lines(along, sums)):
        inner[which] = value[MAXH : ROWS - MAXH] * factors[SCALE_OF[which], 0:1]
        partial[which] = jnp.concatenate([value[:MAXH], value[ROWS - MAXH :]], axis=0)


def within(fitted, sides, across, along, factors):
    return pl.pallas_call(
        within_kernel,
        out_shape=(
            jax.ShapeDtypeStruct((3, INNER, COLS), jnp.float32),
            jax.ShapeDtypeStruct((3, EDGES, COLS), jnp.float32),
        ),
        in_specs=[VMEM] * 5,
        out_specs=(VMEM, VMEM),
        compiler_params=LIMIT,
        cost_estimate=pl.CostEstimate(flops=1 << 27, bytes_accessed=1 << 20, transcendentals=0),
        name="within",
    )(fitted, sides, across, along, factors)


def finish_kernel(across, beyond, factors, fitted, inner, partial, above, below, rate, out, edge, sems):
    writes = [
        pltpu.make_async_copy(fitted, rate, sems.at[0]),
        pltpu.make_async_copy(inner, out.at[:, pl.ds(MAXH, INNER)], sems.at[1]),
        pltpu.make_async_copy(edge.at[:, pl.ds(0, MAXH)], out.at[:, pl.ds(0, MAXH)], sems.at[2]),
        pltpu.make_async_copy(edge.at[:, pl.ds(MAXH, MAXH)], out.at[:, pl.ds(ROWS - MAXH, MAXH)], sems.at[3]),
    ]
    for write in writes[:2]:
        write.start()
    tile = lax.axis_index("tile")
    up = jnp.where(tile > 0, above[...], 0.0)
    down = jnp.where(tile < TILES - 1, below[...], 0.0)
    values = [jnp.concatenate([part[:MAXH], part[MAXH:]], axis=1) for part in (up, down)]
    sums = over_columns(jnp.concatenate(values, axis=0), across[...])
    for which, value in enumerate(over_lines(beyond, sums)):
        edge[which] = (partial[which] + value) * factors[SCALE_OF[which], 0:1]
    for write in writes[2:]:
        write.start()
    for write in writes:
        write.wait()


def finish(across, beyond, factors, fitted, inner, partial, above, below):
    return pl.pallas_call(
        finish_kernel,
        out_shape=(
            jax.ShapeDtypeStruct((ROWS, COLS), jnp.float32),
            jax.ShapeDtypeStruct((3, ROWS, COLS), jnp.float32),
        ),
        in_specs=[VMEM] * 8,
        out_specs=(ANY, ANY),
        scratch_shapes=[pltpu.VMEM((3, EDGES, COLS), jnp.float32), pltpu.SemaphoreType.DMA((4,))],
        compiler_params=LIMIT,
        name="finish",
    )(across, beyond, factors, fitted, inner, partial, above, below)


def per_device(anomaly, mask, epoch_weight, days, window):
    tau = (days.astype(jnp.float32) - 1826.5) / 365.25
    packed = read_packs(STEPS[:1], epoch_weight, anomaly, mask)
    packed += read_packs(STEPS[1:], epoch_weight, anomaly, mask)
    packed += packs((0,), epoch_weight, anomaly, mask)
    got = [shift(values, step, True) for step, values in zip(STEPS, packed)]
    early, times, across, along, beyond, factors = early_sums(tau, window, packed[3], got[0])
    mine = late_sums(times, early, got[1], got[2])
    rest = lax.all_to_all(mine, AXES, split_axis=0, concat_axis=0, tiled=True, axis_index_groups=second_rings())
    fitted, sides, top, bottom = fitted_rate(rest)
    above = lax.ppermute(bottom, "tile", [(i, (i + 1) % TILES) for i in range(TILES)])
    below = lax.ppermute(top, "tile", [(i, (i - 1) % TILES) for i in range(TILES)])
    inner, partial = within(fitted, sides, across, along, factors)
    return finish(across, beyond, factors, fitted, inner, partial, above, below)


def solution(mesh):
    in_specs = (P("epoch", "tile", None), P("epoch", "tile", None), P(), P(), P("tile", "epoch"))
    out_specs = (P("tile", "epoch"), P(None, "tile", "epoch"))
    return jax.shard_map(
        per_device, mesh=mesh, in_specs=in_specs, out_specs=out_specs, check_vma=False
    )
```

```python
import functools

import jax
import jax.numpy as jnp
from jax import lax
from jax.experimental import pallas as pl
from jax.experimental.pallas import tpu as pltpu
from jax.sharding import PartitionSpec as P

MAXH = 16
SIDE = 4
OWN = 4
ROWS = 96
COLS = 128
TILES = 32
AXES = ("epoch", "tile")
STEPS = (2, -1, 1)
ANY = pl.BlockSpec(memory_space=pl.ANY)
SMEM = pl.BlockSpec(memory_space=pltpu.SMEM)
VMEM = pl.BlockSpec(memory_space=pltpu.VMEM)
LIMIT = pltpu.CompilerParams(vmem_limit_bytes=12 << 20)
FIRST_LIMIT = pltpu.CompilerParams(vmem_limit_bytes=62 << 20)
STRIP = 16
BLOCKS = SIDE * SIDE
BESIDE = 2 * MAXH
SLOTS = SIDE + 1
TALL = 6 * ROWS + ROWS // SIDE


def ring_pairs(step, first):
    pairs = []
    for x in range(SIDE):
        for y in range(SIDE):
            for tile in range(TILES):
                if (tile % 2 == 0) == first:
                    there = (x + step) % SIDE * SIDE + y
                else:
                    there = x * SIDE + (y + step) % SIDE
                pairs.append(((x * SIDE + y) * TILES + tile, there * TILES + tile))
    return pairs


def shift(values, step, first):
    return lax.ppermute(values, AXES, ring_pairs(step, first))


def place():
    spot = lax.axis_index("epoch")
    even = lax.axis_index("tile") % 2 == 0
    x, y = spot // SIDE, spot % SIDE
    return jnp.where(even, x, y), jnp.where(even, y, x), even


def block_of(even, first, second):
    return jnp.where(even, SIDE * first + second, SIDE * second + first)


def epoch_of(even, first, second):
    return block_of(even, first, second) * OWN


def columns(block):
    return pl.ds(pl.multiple_of(block * COLS, COLS), COLS)


def lane(shape):
    return lax.broadcasted_iota(jnp.int32, shape, 1)


def group_of(shape):
    return (lane(shape) + MAXH) % COLS // BESIDE


def pack_epoch(step, own, quality, anomaly, mask, out):
    first, second, even = place()
    there = (first + step + SIDE) % SIDE
    weight = quality[epoch_of(even, first, second) + own]
    shape = (ROWS, COLS)
    ahead = lane(shape) < COLS // 2
    group = group_of(shape)
    levels = jnp.zeros(shape, jnp.bfloat16)
    heavies = jnp.zeros(shape, jnp.bfloat16)
    for slot in range(SIDE):
        block = block_of(even, there, slot)
        cols = columns(block)
        before, after = columns(jnp.maximum(block - 1, 0)), columns(jnp.minimum(block + 1, BLOCKS - 1))
        out[slot, own] = anomaly[own, :, cols]
        out[slot, OWN + own] = (mask[own, :, cols].astype(jnp.float32) * weight).astype(jnp.bfloat16)
        level = jnp.where(ahead, anomaly[own, :, after], anomaly[own, :, before])
        valid = jnp.where(ahead, mask[own, :, after], mask[own, :, before]).astype(jnp.float32)
        weights = jnp.where(
            lane((1, COLS)) < COLS // 2,
            jnp.where(block < BLOCKS - 1, weight, 0.0),
            jnp.where(block > 0, weight, 0.0),
        )
        heavy = (valid * weights).astype(jnp.bfloat16)
        if slot:
            level = pltpu.roll(level, slot * BESIDE, 1)
            heavy = pltpu.roll(heavy, slot * BESIDE, 1)
        levels = jnp.where(group == slot, level, levels)
        heavies = jnp.where(group == slot, heavy, heavies)
    out[SIDE, own] = levels
    out[SIDE, OWN + own] = heavies


PACKED = jax.ShapeDtypeStruct((SLOTS, 2 * OWN, ROWS, COLS), jnp.bfloat16)


def read_windows(steps, even, first):
    if len(steps) > 1:
        return (((0, BLOCKS),),) * 2
    there = (first + steps[0] + SIDE) % SIDE
    run = SIDE + 2
    on_even = ((jnp.clip(SIDE * there - 1, 0, BLOCKS - run), run),)
    on_odd = tuple((jnp.clip(SIDE * slot + there - 1, 0, BLOCKS - 3), 3) for slot in range(SIDE))
    return on_even, on_odd


def read_pack_kernel(steps, quality, anomaly, mask, *refs):
    outs, (level, valid, packed, own_quality, sems, done, ready) = refs[: len(steps)], refs[len(steps) :]
    known = pltpu.make_async_copy(quality, own_quality, ready)
    known.start()
    first, second, even = place()
    on_even, on_odd = read_windows(steps, even, first)

    def reads(windows, own):
        for index, (start, blocks) in enumerate(windows):
            cols = pl.ds(pl.multiple_of(start * COLS, COLS), blocks * COLS)
            yield pltpu.make_async_copy(mask.at[own, :, cols], valid.at[own, :, cols], sems.at[own, index, 0])
            yield pltpu.make_async_copy(anomaly.at[own, :, cols], level.at[own, :, cols], sems.at[own, index, 1])

    def on_parity(act):
        if on_even is on_odd:
            act(on_even)
        else:
            pl.when(even)(lambda: act(on_even))
            pl.when(jnp.logical_not(even))(lambda: act(on_odd))

    def start(windows):
        for own in range(OWN):
            for copy in reads(windows, own):
                copy.start()

    on_parity(start)
    known.wait()
    writes = []
    for own in range(OWN):

        def wait(windows):
            for copy in reads(windows, own):
                copy.wait()

        on_parity(wait)
        for index, (step, out) in enumerate(zip(steps, outs)):
            pack_epoch(step, own, own_quality, level, valid, packed.at[index])
            for kind, which in enumerate((own, OWN + own)):
                writes.append(
                    pltpu.make_async_copy(packed.at[index, :, which], out.at[:, which], done.at[index, own, kind])
                )
                writes[-1].start()
    for write in writes:
        write.wait()


def read_packs(steps, quality, anomaly, mask):
    width = COLS * BLOCKS
    return pl.pallas_call(
        functools.partial(read_pack_kernel, steps),
        out_shape=(PACKED,) * len(steps),
        in_specs=[ANY, ANY, ANY],
        out_specs=(ANY,) * len(steps),
        scratch_shapes=[
            pltpu.VMEM((OWN, ROWS, width), jnp.bfloat16),
            pltpu.VMEM((OWN, ROWS, width), jnp.int32),
            pltpu.VMEM((len(steps),) + PACKED.shape, jnp.bfloat16),
            pltpu.SMEM((BLOCKS * OWN,), jnp.float32),
            pltpu.SemaphoreType.DMA((OWN, SIDE, 2)),
            pltpu.SemaphoreType.DMA((len(steps), OWN, 2)),
            pltpu.SemaphoreType.DMA,
        ],
        compiler_params=FIRST_LIMIT,
        cost_estimate=pl.CostEstimate(flops=1 << 20, bytes_accessed=5 << 20, transcendentals=0),
        name="read_pack",
    )(quality, anomaly, mask)


def pack_kernel(steps, quality, anomaly, mask, *outs):
    for step, out in zip(steps, outs):
        for own in range(OWN):
            pack_epoch(step, own, quality, anomaly, mask, out)


def packs(steps, quality, anomaly, mask):
    return pl.pallas_call(
        functools.partial(pack_kernel, steps),
        out_shape=(PACKED,) * len(steps),
        in_specs=[SMEM, VMEM, VMEM],
        out_specs=(VMEM,) * len(steps),
        compiler_params=LIMIT,
        cost_estimate=pl.CostEstimate(flops=1 << 20, bytes_accessed=3 << 20, transcendentals=0),
        name="pack",
    )(quality, anomaly, mask)


def added(totals, heavy, height, moment):
    timed = heavy * moment
    loaded = heavy * height
    terms = (heavy, timed, timed * moment, loaded, loaded * moment)
    return terms if totals is None else tuple(map(jnp.add, totals, terms))


def moments_of(tau, moved):
    first, second, even = place()
    base = epoch_of(even, (first - moved + SIDE) % SIDE, second)
    return [tau[base + own] for own in range(OWN)]


def more(totals, packed, slot, at, moments):
    for own in range(OWN):
        heavy = packed[slot, OWN + own, at].astype(jnp.float32)
        totals = added(totals, heavy, packed[slot, own, at].astype(jnp.float32), moments[own])
    return totals


def over_rows(body):
    for index in range(ROWS // STRIP):
        body(pl.ds(index * STRIP, STRIP))


EDGES = 2 * MAXH
TAPS = 4
TIMES = jax.ShapeDtypeStruct((2, OWN, STRIP, COLS), jnp.float32)
PREPARED = (
    jax.ShapeDtypeStruct((2 * COLS, TAPS * COLS), jnp.bfloat16),
    jax.ShapeDtypeStruct((TAPS, ROWS, ROWS), jnp.bfloat16),
    jax.ShapeDtypeStruct((TAPS, EDGES, EDGES), jnp.bfloat16),
    jax.ShapeDtypeStruct((2, 8, COLS), jnp.float32),
)


def bowl_taps(offset, half):
    return (3 * offset * offset - half * (half + 1)).astype(jnp.float32)


def taps(offset, half):
    inside = jnp.abs(offset) <= half
    flat = jnp.where(inside, 1.0, 0.0).astype(jnp.bfloat16)
    slope = jnp.where(inside, offset, 0).astype(jnp.float32).astype(jnp.bfloat16)
    bowl = jnp.where(inside, bowl_taps(offset, half), 0.0)
    most = bowl.astype(jnp.bfloat16)
    return flat, slope, most, (bowl - most.astype(jnp.float32)).astype(jnp.bfloat16)


def prepare(half, across, along, beyond, factors):
    line = lax.broadcasted_iota(jnp.int32, (2 * COLS, COLS), 0)
    column = jnp.where(line < COLS + MAXH, line, jnp.where(line >= 2 * COLS - MAXH, line - 2 * COLS, 4 * COLS))
    across[...] = jnp.concatenate(taps(column - lane((2 * COLS, COLS)), half), axis=1)
    shape = (ROWS, ROWS)
    for which, tap in enumerate(taps(lane(shape) - lax.broadcasted_iota(jnp.int32, shape, 0), half)):
        along[which] = tap
    shape = (EDGES, EDGES)
    spot = lane(shape)
    mine = lax.broadcasted_iota(jnp.int32, shape, 0)
    row = jnp.where(spot < MAXH, spot - MAXH, spot + ROWS - MAXH)
    mine = jnp.where(mine < MAXH, mine, mine + ROWS - EDGES)
    for which, tap in enumerate(taps(row - mine, half)):
        beyond[which] = tap
    width = half.astype(jnp.float32)
    taps_at = lane((8, COLS)) - MAXH
    inside = jnp.abs(taps_at) <= half
    squares = (taps_at * taps_at).astype(jnp.float32)
    bowls = bowl_taps(taps_at, half)
    slope_norm = jnp.sum(jnp.where(inside, squares, 0.0), axis=1, keepdims=True)
    bowl_norm = jnp.sum(jnp.where(inside, bowls * bowls, 0.0), axis=1, keepdims=True)
    shape = (8, COLS)
    factors[0] = jnp.broadcast_to(6.0 * width * width / ((2.0 * width + 1.0) * bowl_norm), shape)
    factors[1] = jnp.broadcast_to(width * width / (slope_norm * slope_norm), shape)


def early_kernel(tau, window, own, got, out, times, *prepared):
    near, far = moments_of(tau, 0), moments_of(tau, STEPS[0])
    for index, moved in enumerate(STEPS[1:]):
        for which, moment in enumerate(moments_of(tau, moved)):
            times[index, which] = jnp.full((STRIP, COLS), moment, jnp.float32)
    for slot in range(SLOTS):

        def body(at):
            totals = more(more(None, own, slot, at, near), got, slot, at, far)
            for which, total in enumerate(totals):
                out[slot, which, at] = total

        over_rows(body)
    prepare(window[0, 0], *prepared)


def early_sums(tau, window, own, got):
    return pl.pallas_call(
        early_kernel,
        out_shape=(jax.ShapeDtypeStruct((SLOTS, 5, ROWS, COLS), jnp.float32), TIMES) + PREPARED,
        in_specs=[SMEM, SMEM, VMEM, VMEM],
        out_specs=(VMEM,) * 6,
        compiler_params=LIMIT,
        cost_estimate=pl.CostEstimate(flops=1 << 23, bytes_accessed=3 << 20, transcendentals=0),
        name="early",
    )(tau, window, own, got)


def middle_kernel(times, early, got, out):
    for slot in range(SLOTS):

        def body(at):
            totals = tuple(early[slot, which, at] for which in range(5))
            totals = more(totals, got, slot, at, [times[0, own] for own in range(OWN)])
            for which, total in enumerate(totals):
                out[slot, which, at] = total

        over_rows(body)


def middle_sums(times, early, got):
    return pl.pallas_call(
        middle_kernel,
        out_shape=jax.ShapeDtypeStruct((SLOTS, 5, ROWS, COLS), jnp.float32),
        in_specs=[VMEM, VMEM, VMEM],
        out_specs=VMEM,
        compiler_params=LIMIT,
        cost_estimate=pl.CostEstimate(flops=1 << 22, bytes_accessed=4 << 20, transcendentals=0),
        name="middle",
    )(times, early, got)


def late_kernel(times, early, got, out, beside):
    moments = [times[1, own] for own in range(OWN)]

    def total_of(slot, at):
        totals = tuple(early[slot, which, at] for which in range(5))
        return more(totals, got, slot, at, moments)

    for slot in (SIDE,) + tuple(range(SIDE)):

        def body(at):
            for which, total in enumerate(total_of(slot, at)):
                if slot < SIDE:
                    out[slot, pl.ds(which * ROWS + at.start, STRIP)] = total
                else:
                    beside[which, at] = total

        over_rows(body)
    quarter = ROWS // SIDE
    group = group_of((ROWS, COLS))
    short = group_of((quarter, COLS))

    def turned(values, count):
        return pltpu.roll(values, count % SIDE * BESIDE, 1) if count % SIDE else values

    for slot in range(SIDE):
        full = jnp.zeros((ROWS, COLS), jnp.float32)
        part = jnp.zeros((quarter, COLS), jnp.float32)
        for which in range(SIDE):
            full = jnp.where(group == which, turned(beside[which], which - slot), full)
            piece = beside[4, pl.ds(which * quarter, quarter)]
            part = jnp.where(short == which, turned(piece, which - slot), part)
        out[slot, pl.ds(5 * ROWS, ROWS)] = full
        out[slot, pl.ds(6 * ROWS, quarter)] = part


def late_sums(times, early, got):
    return pl.pallas_call(
        late_kernel,
        out_shape=jax.ShapeDtypeStruct((SIDE, TALL, COLS), jnp.float32),
        in_specs=[VMEM, VMEM, VMEM],
        out_specs=VMEM,
        scratch_shapes=[pltpu.VMEM((5, ROWS, COLS), jnp.float32)],
        compiler_params=LIMIT,
        cost_estimate=pl.CostEstimate(flops=1 << 23, bytes_accessed=4 << 20, transcendentals=0),
        name="late",
    )(times, early, got)


def second_rings():
    rings = []
    for tile in range(TILES):
        for fixed in range(SIDE):
            spots = [fixed * SIDE + i if tile % 2 == 0 else i * SIDE + fixed for i in range(SIDE)]
            rings.append([spot * TILES + tile for spot in spots])
    return rings


def slope_from(sums):
    lifted = sums[0] + 1.0
    return (lifted * sums[4] - sums[1] * sums[3]) / (lifted * (sums[2] + 1.0) - sums[1] * sums[1])


def rate_kernel(got, rate, sides, top, bottom):
    total = got[0] + got[1] + got[2] + got[3]
    value = slope_from([total[which * ROWS : (which + 1) * ROWS] for which in range(5)])
    full = total[5 * ROWS : 6 * ROWS]
    part = total[6 * ROWS :]

    def back(values, which):
        return pltpu.roll(values, COLS - which * BESIDE, 1) if which else values

    spread = [back(full, which) for which in range(4)]
    spread.append(jnp.concatenate([back(part, which) for which in range(SIDE)], axis=0))
    beside = jnp.where(group_of((ROWS, COLS)) == 0, slope_from(spread), 0.0)
    rate[...] = value
    sides[...] = beside
    top[...] = jnp.concatenate([value[:MAXH], beside[:MAXH]], axis=0)
    bottom[...] = jnp.concatenate([value[ROWS - MAXH :], beside[ROWS - MAXH :]], axis=0)


def fitted_rate(got):
    block = jax.ShapeDtypeStruct((ROWS, COLS), jnp.float32)
    edge = jax.ShapeDtypeStruct((2 * MAXH, COLS), jnp.float32)
    return pl.pallas_call(
        rate_kernel,
        out_shape=(block, block, edge, edge),
        in_specs=[VMEM],
        out_specs=(VMEM,) * 4,
        compiler_params=LIMIT,
        name="rate",
    )(got)


def three_parts(values):
    high = values.astype(jnp.bfloat16)
    rest = values - high.astype(jnp.float32)
    middle = rest.astype(jnp.bfloat16)
    low = (rest - middle.astype(jnp.float32)).astype(jnp.bfloat16)
    return high, middle, low


def product(left, right):
    return jnp.dot(left, right, preferred_element_type=jnp.float32)


def over_columns(values, across):
    parts = three_parts(values)
    wide = product(parts[0], across) + product(parts[1], across) + product(parts[2], across)
    flat, slope, most, rest = (wide[:, i * COLS : (i + 1) * COLS] for i in range(TAPS))
    return flat, slope, most + rest


def over_lines(along, sums):
    flat, slope, bowl = sums

    def down(weights, values):
        a, b, c = (product(weights, part) for part in three_parts(values))
        return a + b + c

    return down(along[0], bowl), down(along[2], flat) + down(along[3], flat), down(along[1], slope)


SCALE_OF = (0, 0, 1)
INNER = ROWS - EDGES


def within_kernel(fitted, sides, across, along, factors, inner, partial):
    sums = over_columns(jnp.concatenate([fitted[...], sides[...]], axis=1), across[...])
    for which, value in enumerate(over_lines(along, sums)):
        inner[which] = value[MAXH : ROWS - MAXH] * factors[SCALE_OF[which], 0:1]
        partial[which] = jnp.concatenate([value[:MAXH], value[ROWS - MAXH :]], axis=0)


def within(fitted, sides, across, along, factors):
    return pl.pallas_call(
        within_kernel,
        out_shape=(
            jax.ShapeDtypeStruct((3, INNER, COLS), jnp.float32),
            jax.ShapeDtypeStruct((3, EDGES, COLS), jnp.float32),
        ),
        in_specs=[VMEM] * 5,
        out_specs=(VMEM, VMEM),
        compiler_params=LIMIT,
        cost_estimate=pl.CostEstimate(flops=1 << 27, bytes_accessed=1 << 20, transcendentals=0),
        name="within",
    )(fitted, sides, across, along, factors)


def finish_kernel(across, beyond, factors, fitted, inner, partial, above, below, rate, out, edge, sems):
    writes = [
        pltpu.make_async_copy(fitted, rate, sems.at[0]),
        pltpu.make_async_copy(inner, out.at[:, pl.ds(MAXH, INNER)], sems.at[1]),
    ]
    for write in writes:
        write.start()
    tile = lax.axis_index("tile")
    up = jnp.where(tile > 0, above[...], 0.0)
    down = jnp.where(tile < TILES - 1, below[...], 0.0)
    values = [jnp.concatenate([part[:MAXH], part[MAXH:]], axis=1) for part in (up, down)]
    sums = over_columns(jnp.concatenate(values, axis=0), across[...])
    for which, value in enumerate(over_lines(beyond, sums)):
        edge[which] = (partial[which] + value) * factors[SCALE_OF[which], 0:1]
        for end, row in enumerate((0, ROWS - MAXH)):
            write = pltpu.make_async_copy(
                edge.at[which, pl.ds(end * MAXH, MAXH)], out.at[which, pl.ds(row, MAXH)], sems.at[2 + 2 * which + end]
            )
            write.start()
            writes.append(write)
    for write in writes:
        write.wait()


def finish(across, beyond, factors, fitted, inner, partial, above, below):
    return pl.pallas_call(
        finish_kernel,
        out_shape=(
            jax.ShapeDtypeStruct((ROWS, COLS), jnp.float32),
            jax.ShapeDtypeStruct((3, ROWS, COLS), jnp.float32),
        ),
        in_specs=[VMEM] * 8,
        out_specs=(ANY, ANY),
        scratch_shapes=[pltpu.VMEM((3, EDGES, COLS), jnp.float32), pltpu.SemaphoreType.DMA((8,))],
        compiler_params=LIMIT,
        name="finish",
    )(across, beyond, factors, fitted, inner, partial, above, below)


def per_device(anomaly, mask, epoch_weight, days, window):
    tau = (days.astype(jnp.float32) - 1826.5) / 365.25
    packed = read_packs(STEPS[:1], epoch_weight, anomaly, mask)
    packed += read_packs(STEPS[1:], epoch_weight, anomaly, mask)
    packed += packs((0,), epoch_weight, anomaly, mask)
    got = [shift(values, step, True) for step, values in zip(STEPS, packed)]
    early, times, across, along, beyond, factors = early_sums(tau, window, packed[3], got[0])
    middle = middle_sums(times, early, got[1])
    mine = late_sums(times, middle, got[2])
    rest = lax.all_to_all(mine, AXES, split_axis=0, concat_axis=0, tiled=True, axis_index_groups=second_rings())
    fitted, sides, top, bottom = fitted_rate(rest)
    above = lax.ppermute(bottom, "tile", [(i, (i + 1) % TILES) for i in range(TILES)])
    below = lax.ppermute(top, "tile", [(i, (i - 1) % TILES) for i in range(TILES)])
    inner, partial = within(fitted, sides, across, along, factors)
    return finish(across, beyond, factors, fitted, inner, partial, above, below)


def solution(mesh):
    in_specs = (P("epoch", "tile", None), P("epoch", "tile", None), P(), P(), P("tile", "epoch"))
    out_specs = (P("tile", "epoch"), P(None, "tile", "epoch"))
    return jax.shard_map(
        per_device, mesh=mesh, in_specs=in_specs, out_specs=out_specs, check_vma=False
    )
```

```python
import functools

import jax
import jax.numpy as jnp
from jax import lax
from jax.experimental import pallas as pl
from jax.experimental.pallas import tpu as pltpu
from jax.sharding import PartitionSpec as P

MAXH = 16
SIDE = 4
OWN = 4
ROWS = 96
COLS = 128
TILES = 32
AXES = ("epoch", "tile")
STEPS = (2, -1, 1)
ANY = pl.BlockSpec(memory_space=pl.ANY)
SMEM = pl.BlockSpec(memory_space=pltpu.SMEM)
VMEM = pl.BlockSpec(memory_space=pltpu.VMEM)
LIMIT = pltpu.CompilerParams(vmem_limit_bytes=12 << 20)
FIRST_LIMIT = pltpu.CompilerParams(vmem_limit_bytes=62 << 20)
STRIP = 16
BLOCKS = SIDE * SIDE
BESIDE = 2 * MAXH
SLOTS = SIDE + 1
TALL = 6 * ROWS + ROWS // SIDE


def ring_pairs(step, first):
    pairs = []
    for x in range(SIDE):
        for y in range(SIDE):
            for tile in range(TILES):
                if (tile % 2 == 0) == first:
                    there = (x + step) % SIDE * SIDE + y
                else:
                    there = x * SIDE + (y + step) % SIDE
                pairs.append(((x * SIDE + y) * TILES + tile, there * TILES + tile))
    return pairs


def shift(values, step, first):
    return lax.ppermute(values, AXES, ring_pairs(step, first))


def place():
    spot = lax.axis_index("epoch")
    even = lax.axis_index("tile") % 2 == 0
    x, y = spot // SIDE, spot % SIDE
    return jnp.where(even, x, y), jnp.where(even, y, x), even


def block_of(even, first, second):
    return jnp.where(even, SIDE * first + second, SIDE * second + first)


def epoch_of(even, first, second):
    return block_of(even, first, second) * OWN


def columns(block):
    return pl.ds(pl.multiple_of(block * COLS, COLS), COLS)


def lane(shape):
    return lax.broadcasted_iota(jnp.int32, shape, 1)


def group_of(shape):
    return (lane(shape) + MAXH) % COLS // BESIDE


def pack_epoch(step, own, quality, anomaly, mask, out):
    first, second, even = place()
    there = (first + step + SIDE) % SIDE
    weight = quality[epoch_of(even, first, second) + own]
    shape = (ROWS, COLS)
    ahead = lane(shape) < COLS // 2
    group = group_of(shape)
    levels = jnp.zeros(shape, jnp.bfloat16)
    heavies = jnp.zeros(shape, jnp.bfloat16)
    for slot in range(SIDE):
        block = block_of(even, there, slot)
        cols = columns(block)
        before, after = columns(jnp.maximum(block - 1, 0)), columns(jnp.minimum(block + 1, BLOCKS - 1))
        out[slot, own] = anomaly[own, :, cols]
        out[slot, OWN + own] = (mask[own, :, cols].astype(jnp.float32) * weight).astype(jnp.bfloat16)
        level = jnp.where(ahead, anomaly[own, :, after], anomaly[own, :, before])
        valid = jnp.where(ahead, mask[own, :, after], mask[own, :, before]).astype(jnp.float32)
        weights = jnp.where(
            lane((1, COLS)) < COLS // 2,
            jnp.where(block < BLOCKS - 1, weight, 0.0),
            jnp.where(block > 0, weight, 0.0),
        )
        heavy = (valid * weights).astype(jnp.bfloat16)
        if slot:
            level = pltpu.roll(level, slot * BESIDE, 1)
            heavy = pltpu.roll(heavy, slot * BESIDE, 1)
        levels = jnp.where(group == slot, level, levels)
        heavies = jnp.where(group == slot, heavy, heavies)
    out[SIDE, own] = levels
    out[SIDE, OWN + own] = heavies


PACKED = jax.ShapeDtypeStruct((SLOTS, 2 * OWN, ROWS, COLS), jnp.bfloat16)


def read_windows(steps, even, first):
    if len(steps) > 1:
        return (((0, BLOCKS),),) * 2
    there = (first + steps[0] + SIDE) % SIDE
    run = SIDE + 2
    on_even = ((jnp.clip(SIDE * there - 1, 0, BLOCKS - run), run),)
    on_odd = tuple((jnp.clip(SIDE * slot + there - 1, 0, BLOCKS - 3), 3) for slot in range(SIDE))
    return on_even, on_odd


def read_pack_kernel(steps, quality, anomaly, mask, *refs):
    outs, (level, valid, packed, own_quality, sems, done, ready) = refs[: len(steps)], refs[len(steps) :]
    known = pltpu.make_async_copy(quality, own_quality, ready)
    known.start()
    first, second, even = place()
    on_even, on_odd = read_windows(steps, even, first)

    def reads(windows, own):
        for index, (start, blocks) in enumerate(windows):
            cols = pl.ds(pl.multiple_of(start * COLS, COLS), blocks * COLS)
            yield pltpu.make_async_copy(mask.at[own, :, cols], valid.at[own, :, cols], sems.at[own, index, 0])
            yield pltpu.make_async_copy(anomaly.at[own, :, cols], level.at[own, :, cols], sems.at[own, index, 1])

    def on_parity(act):
        if on_even is on_odd:
            act(on_even)
        else:
            pl.when(even)(lambda: act(on_even))
            pl.when(jnp.logical_not(even))(lambda: act(on_odd))

    def start(windows):
        for own in range(OWN):
            for copy in reads(windows, own):
                copy.start()

    on_parity(start)
    known.wait()
    writes = []
    for own in range(OWN):

        def wait(windows):
            for copy in reads(windows, own):
                copy.wait()

        on_parity(wait)
        for index, (step, out) in enumerate(zip(steps, outs)):
            pack_epoch(step, own, own_quality, level, valid, packed.at[index])
            for kind, which in enumerate((own, OWN + own)):
                writes.append(
                    pltpu.make_async_copy(packed.at[index, :, which], out.at[:, which], done.at[index, own, kind])
                )
                writes[-1].start()
    for write in writes:
        write.wait()


def read_packs(steps, quality, anomaly, mask):
    width = COLS * BLOCKS
    return pl.pallas_call(
        functools.partial(read_pack_kernel, steps),
        out_shape=(PACKED,) * len(steps),
        in_specs=[ANY, ANY, ANY],
        out_specs=(ANY,) * len(steps),
        scratch_shapes=[
            pltpu.VMEM((OWN, ROWS, width), jnp.bfloat16),
            pltpu.VMEM((OWN, ROWS, width), jnp.int32),
            pltpu.VMEM((len(steps),) + PACKED.shape, jnp.bfloat16),
            pltpu.SMEM((BLOCKS * OWN,), jnp.float32),
            pltpu.SemaphoreType.DMA((OWN, SIDE, 2)),
            pltpu.SemaphoreType.DMA((len(steps), OWN, 2)),
            pltpu.SemaphoreType.DMA,
        ],
        compiler_params=FIRST_LIMIT,
        cost_estimate=pl.CostEstimate(flops=1 << 20, bytes_accessed=5 << 20, transcendentals=0),
        name="read_pack",
    )(quality, anomaly, mask)


def pack_kernel(steps, quality, anomaly, mask, *outs):
    for step, out in zip(steps, outs):
        for own in range(OWN):
            pack_epoch(step, own, quality, anomaly, mask, out)


def packs(steps, quality, anomaly, mask):
    return pl.pallas_call(
        functools.partial(pack_kernel, steps),
        out_shape=(PACKED,) * len(steps),
        in_specs=[SMEM, VMEM, VMEM],
        out_specs=(VMEM,) * len(steps),
        compiler_params=LIMIT,
        cost_estimate=pl.CostEstimate(flops=1 << 20, bytes_accessed=3 << 20, transcendentals=0),
        name="pack",
    )(quality, anomaly, mask)


def added(totals, heavy, height, moment):
    timed = heavy * moment
    loaded = heavy * height
    terms = (heavy, timed, timed * moment, loaded, loaded * moment)
    return terms if totals is None else tuple(map(jnp.add, totals, terms))


def moments_of(tau, moved):
    first, second, even = place()
    base = epoch_of(even, (first - moved + SIDE) % SIDE, second)
    return [tau[base + own] for own in range(OWN)]


def more(totals, packed, slot, at, moments):
    for own in range(OWN):
        heavy = packed[slot, OWN + own, at].astype(jnp.float32)
        totals = added(totals, heavy, packed[slot, own, at].astype(jnp.float32), moments[own])
    return totals


def over_rows(body):
    for index in range(ROWS // STRIP):
        body(pl.ds(index * STRIP, STRIP))


EDGES = 2 * MAXH
TAPS = 4
TIMES = jax.ShapeDtypeStruct((2, OWN, STRIP, COLS), jnp.float32)
PREPARED = (
    jax.ShapeDtypeStruct((2 * COLS, TAPS * COLS), jnp.bfloat16),
    jax.ShapeDtypeStruct((TAPS, ROWS, ROWS), jnp.bfloat16),
    jax.ShapeDtypeStruct((TAPS, EDGES, EDGES), jnp.bfloat16),
    jax.ShapeDtypeStruct((2, 8, COLS), jnp.float32),
)


def bowl_taps(offset, half):
    return (3 * offset * offset - half * (half + 1)).astype(jnp.float32)


def taps(offset, half):
    inside = jnp.abs(offset) <= half
    flat = jnp.where(inside, 1.0, 0.0).astype(jnp.bfloat16)
    slope = jnp.where(inside, offset, 0).astype(jnp.float32).astype(jnp.bfloat16)
    bowl = jnp.where(inside, bowl_taps(offset, half), 0.0)
    most = bowl.astype(jnp.bfloat16)
    return flat, slope, most, (bowl - most.astype(jnp.float32)).astype(jnp.bfloat16)


def prepare(half, across, along, beyond, factors):
    line = lax.broadcasted_iota(jnp.int32, (2 * COLS, COLS), 0)
    column = jnp.where(line < COLS + MAXH, line, jnp.where(line >= 2 * COLS - MAXH, line - 2 * COLS, 4 * COLS))
    across[...] = jnp.concatenate(taps(column - lane((2 * COLS, COLS)), half), axis=1)
    shape = (ROWS, ROWS)
    for which, tap in enumerate(taps(lane(shape) - lax.broadcasted_iota(jnp.int32, shape, 0), half)):
        along[which] = tap
    shape = (EDGES, EDGES)
    spot = lane(shape)
    mine = lax.broadcasted_iota(jnp.int32, shape, 0)
    row = jnp.where(spot < MAXH, spot - MAXH, spot + ROWS - MAXH)
    mine = jnp.where(mine < MAXH, mine, mine + ROWS - EDGES)
    for which, tap in enumerate(taps(row - mine, half)):
        beyond[which] = tap
    width = half.astype(jnp.float32)
    taps_at = lane((8, COLS)) - MAXH
    inside = jnp.abs(taps_at) <= half
    squares = (taps_at * taps_at).astype(jnp.float32)
    bowls = bowl_taps(taps_at, half)
    slope_norm = jnp.sum(jnp.where(inside, squares, 0.0), axis=1, keepdims=True)
    bowl_norm = jnp.sum(jnp.where(inside, bowls * bowls, 0.0), axis=1, keepdims=True)
    shape = (8, COLS)
    factors[0] = jnp.broadcast_to(6.0 * width * width / ((2.0 * width + 1.0) * bowl_norm), shape)
    factors[1] = jnp.broadcast_to(width * width / (slope_norm * slope_norm), shape)


def early_kernel(tau, window, own, got, out, times, *prepared):
    near, far = moments_of(tau, 0), moments_of(tau, STEPS[0])
    for index, moved in enumerate(STEPS[1:]):
        for which, moment in enumerate(moments_of(tau, moved)):
            times[index, which] = jnp.full((STRIP, COLS), moment, jnp.float32)
    for slot in range(SLOTS):

        def body(at):
            totals = more(more(None, own, slot, at, near), got, slot, at, far)
            for which, total in enumerate(totals):
                out[slot, which, at] = total

        over_rows(body)
    prepare(window[0, 0], *prepared)


def early_sums(tau, window, own, got):
    return pl.pallas_call(
        early_kernel,
        out_shape=(jax.ShapeDtypeStruct((SLOTS, 5, ROWS, COLS), jnp.float32), TIMES) + PREPARED,
        in_specs=[SMEM, SMEM, VMEM, VMEM],
        out_specs=(VMEM,) * 6,
        compiler_params=LIMIT,
        cost_estimate=pl.CostEstimate(flops=1 << 23, bytes_accessed=3 << 20, transcendentals=0),
        name="early",
    )(tau, window, own, got)


def middle_kernel(times, early, got, out):
    for slot in range(SLOTS):

        def body(at):
            totals = tuple(early[slot, which, at] for which in range(5))
            totals = more(totals, got, slot, at, [times[0, own] for own in range(OWN)])
            for which, total in enumerate(totals):
                out[slot, which, at] = total

        over_rows(body)


def middle_sums(times, early, got):
    return pl.pallas_call(
        middle_kernel,
        out_shape=jax.ShapeDtypeStruct((SLOTS, 5, ROWS, COLS), jnp.float32),
        in_specs=[VMEM, VMEM, VMEM],
        out_specs=VMEM,
        compiler_params=LIMIT,
        cost_estimate=pl.CostEstimate(flops=1 << 22, bytes_accessed=4 << 20, transcendentals=0),
        name="middle",
    )(times, early, got)


def late_kernel(times, early, got, out, beside):
    moments = [times[1, own] for own in range(OWN)]

    def total_of(slot, at):
        totals = tuple(early[slot, which, at] for which in range(5))
        return more(totals, got, slot, at, moments)

    for slot in (SIDE,) + tuple(range(SIDE)):

        def body(at):
            for which, total in enumerate(total_of(slot, at)):
                if slot < SIDE:
                    out[slot, pl.ds(which * ROWS + at.start, STRIP)] = total
                else:
                    beside[which, at] = total

        over_rows(body)
    quarter = ROWS // SIDE
    group = group_of((ROWS, COLS))
    short = group_of((quarter, COLS))

    def turned(values, count):
        return pltpu.roll(values, count % SIDE * BESIDE, 1) if count % SIDE else values

    for slot in range(SIDE):
        full = jnp.zeros((ROWS, COLS), jnp.float32)
        part = jnp.zeros((quarter, COLS), jnp.float32)
        for which in range(SIDE):
            full = jnp.where(group == which, turned(beside[which], which - slot), full)
            piece = beside[4, pl.ds(which * quarter, quarter)]
            part = jnp.where(short == which, turned(piece, which - slot), part)
        out[slot, pl.ds(5 * ROWS, ROWS)] = full
        out[slot, pl.ds(6 * ROWS, quarter)] = part


def late_sums(times, early, got):
    return pl.pallas_call(
        late_kernel,
        out_shape=jax.ShapeDtypeStruct((SIDE, TALL, COLS), jnp.float32),
        in_specs=[VMEM, VMEM, VMEM],
        out_specs=VMEM,
        scratch_shapes=[pltpu.VMEM((5, ROWS, COLS), jnp.float32)],
        compiler_params=LIMIT,
        cost_estimate=pl.CostEstimate(flops=1 << 23, bytes_accessed=4 << 20, transcendentals=0),
        name="late",
    )(times, early, got)


def second_rings():
    rings = []
    for tile in range(TILES):
        for fixed in range(SIDE):
            spots = [fixed * SIDE + i if tile % 2 == 0 else i * SIDE + fixed for i in range(SIDE)]
            rings.append([spot * TILES + tile for spot in spots])
    return rings


def slope_from(sums):
    lifted = sums[0] + 1.0
    return (lifted * sums[4] - sums[1] * sums[3]) / (lifted * (sums[2] + 1.0) - sums[1] * sums[1])


def rate_kernel(got, rate, sides, top, bottom):
    total = got[0] + got[1] + got[2] + got[3]
    value = slope_from([total[which * ROWS : (which + 1) * ROWS] for which in range(5)])
    full = total[5 * ROWS : 6 * ROWS]
    part = total[6 * ROWS :]

    def back(values, which):
        return pltpu.roll(values, COLS - which * BESIDE, 1) if which else values

    spread = [back(full, which) for which in range(4)]
    spread.append(jnp.concatenate([back(part, which) for which in range(SIDE)], axis=0))
    beside = jnp.where(group_of((ROWS, COLS)) == 0, slope_from(spread), 0.0)
    rate[...] = value
    sides[...] = beside
    top[...] = jnp.concatenate([value[:MAXH], beside[:MAXH]], axis=0)
    bottom[...] = jnp.concatenate([value[ROWS - MAXH :], beside[ROWS - MAXH :]], axis=0)


def fitted_rate(got):
    block = jax.ShapeDtypeStruct((ROWS, COLS), jnp.float32)
    edge = jax.ShapeDtypeStruct((2 * MAXH, COLS), jnp.float32)
    return pl.pallas_call(
        rate_kernel,
        out_shape=(block, block, edge, edge),
        in_specs=[VMEM],
        out_specs=(VMEM,) * 4,
        compiler_params=LIMIT,
        name="rate",
    )(got)


def three_parts(values):
    high = values.astype(jnp.bfloat16)
    rest = values - high.astype(jnp.float32)
    middle = rest.astype(jnp.bfloat16)
    low = (rest - middle.astype(jnp.float32)).astype(jnp.bfloat16)
    return high, middle, low


def product(left, right):
    return jnp.dot(left, right, preferred_element_type=jnp.float32)


def over_columns(values, across):
    parts = three_parts(values)
    wide = product(parts[0], across) + product(parts[1], across) + product(parts[2], across)
    flat, slope, most, rest = (wide[:, i * COLS : (i + 1) * COLS] for i in range(TAPS))
    return flat, slope, most + rest


def over_lines(along, sums):
    flat, slope, bowl = sums

    def down(weights, values):
        a, b, c = (product(weights, part) for part in three_parts(values))
        return a + b + c

    return down(along[0], bowl), down(along[2], flat) + down(along[3], flat), down(along[1], slope)


SCALE_OF = (0, 0, 1)
INNER = ROWS - EDGES


def within_kernel(fitted, sides, across, along, factors, inner, partial):
    sums = over_columns(jnp.concatenate([fitted[...], sides[...]], axis=1), across[...])
    for which, value in enumerate(over_lines(along, sums)):
        inner[which] = value[MAXH : ROWS - MAXH] * factors[SCALE_OF[which], 0:1]
        partial[which] = jnp.concatenate([value[:MAXH], value[ROWS - MAXH :]], axis=0)


def within(fitted, sides, across, along, factors):
    return pl.pallas_call(
        within_kernel,
        out_shape=(
            jax.ShapeDtypeStruct((3, INNER, COLS), jnp.float32),
            jax.ShapeDtypeStruct((3, EDGES, COLS), jnp.float32),
        ),
        in_specs=[VMEM] * 5,
        out_specs=(VMEM, VMEM),
        compiler_params=LIMIT,
        cost_estimate=pl.CostEstimate(flops=1 << 27, bytes_accessed=1 << 20, transcendentals=0),
        name="within",
    )(fitted, sides, across, along, factors)


def finish_kernel(across, beyond, factors, fitted, inner, partial, above, below, rate, out, edge, sems):
    writes = [
        pltpu.make_async_copy(fitted, rate, sems.at[0]),
        pltpu.make_async_copy(inner, out.at[:, pl.ds(MAXH, INNER)], sems.at[1]),
    ]
    for write in writes:
        write.start()
    tile = lax.axis_index("tile")
    up = jnp.where(tile > 0, above[...], 0.0)
    down = jnp.where(tile < TILES - 1, below[...], 0.0)
    values = [jnp.concatenate([part[:MAXH], part[MAXH:]], axis=1) for part in (up, down)]
    sums = over_columns(jnp.concatenate(values, axis=0), across[...])
    for which, value in enumerate(over_lines(beyond, sums)):
        edge[which] = (partial[which] + value) * factors[SCALE_OF[which], 0:1]
        for end, row in enumerate((0, ROWS - MAXH)):
            write = pltpu.make_async_copy(
                edge.at[which, pl.ds(end * MAXH, MAXH)], out.at[which, pl.ds(row, MAXH)], sems.at[2 + 2 * which + end]
            )
            write.start()
            writes.append(write)
    for write in writes:
        write.wait()


def finish(across, beyond, factors, fitted, inner, partial, above, below):
    return pl.pallas_call(
        finish_kernel,
        out_shape=(
            jax.ShapeDtypeStruct((ROWS, COLS), jnp.float32),
            jax.ShapeDtypeStruct((3, ROWS, COLS), jnp.float32),
        ),
        in_specs=[VMEM] * 8,
        out_specs=(ANY, ANY),
        scratch_shapes=[pltpu.VMEM((3, EDGES, COLS), jnp.float32), pltpu.SemaphoreType.DMA((8,))],
        compiler_params=LIMIT,
        name="finish",
    )(across, beyond, factors, fitted, inner, partial, above, below)


def per_device(anomaly, mask, epoch_weight, days, window):
    tau = (days.astype(jnp.float32) - 1826.5) / 365.25
    packed = read_packs(STEPS[:1], epoch_weight, anomaly, mask)
    packed += read_packs(STEPS[1:], epoch_weight, anomaly, mask)
    packed += packs((0,), epoch_weight, anomaly, mask)
    got = [shift(values, step, True) for step, values in zip(STEPS, packed)]
    early, times, across, along, beyond, factors = early_sums(tau, window, packed[3], got[0])
    middle = middle_sums(times, early, got[1])
    mine = late_sums(times, middle, got[2])
    rest = lax.all_to_all(mine, AXES, split_axis=0, concat_axis=0, tiled=True, axis_index_groups=second_rings())
    fitted, sides, top, bottom = fitted_rate(rest)
    below = lax.ppermute(top, "tile", [(i, (i - 1) % TILES) for i in range(TILES)])
    above = lax.ppermute(bottom, "tile", [(i, (i + 1) % TILES) for i in range(TILES)])
    inner, partial = within(fitted, sides, across, along, factors)
    return finish(across, beyond, factors, fitted, inner, partial, above, below)


def solution(mesh):
    in_specs = (P("epoch", "tile", None), P("epoch", "tile", None), P(), P(), P("tile", "epoch"))
    out_specs = (P("tile", "epoch"), P(None, "tile", "epoch"))
    return jax.shard_map(
        per_device, mesh=mesh, in_specs=in_specs, out_specs=out_specs, check_vma=False
    )
```
